512 devices in a mesh: lat: 32 (over x_hi, z, core), lev: 16 (over y, x_lo).
Axes of the slice: x: 4 (x_hi: 2, x_lo: 2; x = x_hi * 2 + x_lo), y: 8, z: 8, core: 2. Of those that a mesh axis runs over, the one named last changes fastest.
Arguments:
- wind_east: float32 [128, 128, 1152], P('lat', 'lev'), may hold values from -6 to 6
- wind_north: float32 [128, 128, 1152], P('lat', 'lev'), may hold values from -6 to 6
- pot_temp: float32 [128, 128, 1152], P('lat', 'lev'), may hold values from 0.5 to 2
- thickness: float32 [128, 128, 1152], P('lat', 'lev'), may hold values from 0.5 to 1.5
- source_level: int32 [128, 128, 1152], P('lat', 'lev'), may hold values from 0 to 127, as said below
- fraction: float32 [128, 128, 1152], P('lat', 'lev'), may hold values from 0 to 1
Outputs:
- east_content: float32 [128, 128, 1152], P('lat', 'lev')
- north_content: float32 [128, 128, 1152], P('lat', 'lev')
- heat_content: float32 [128, 128, 1152], P('lat', 'lev')
- new_thickness: float32 [128, 128, 1152], P('lat', 'lev')
The draws below stay inside these ranges and needn't reach their ends.
Inputs may be any that keep to these rules, and one draw needn't show every extreme that they name: source_level at level k differs from k by at most 2; it is 0 at level 0 and 127 at the last level.
All inputs are finite; a program needn't handle non-finite values.
Results may differ from the reference program's by a relative error of at most 0.00011.
Values sent between devices are 32-bit elements; how exact they have to be, the bound alone decides.
No kernel may reach another device: no remote copies, remote signals or barrier semaphores. Data moves between devices by JAX's collectives and lax.ppermute only.
A program may use at most 64 MiB of HBM per device.

```python
import math
import jax
import jax.numpy as jnp

LON = 1152
STEPS = 4
LAT = 128
LEVELS = 128


def draw_source_level(key, part):
    key = jax.random.fold_in(key, 11)
    offset = jax.random.randint(key, (LAT, LEVELS, LON), -2, 3)
    level_index = jnp.arange(LEVELS, dtype=jnp.int32)[None, :, None]
    target = jnp.clip(level_index + offset, 0, LEVELS - 1)
    target = jnp.where(level_index == 0, 0, target)
    target = jnp.where(level_index == LEVELS - 1, LEVELS - 1, target)
    return target.astype(jnp.int32)


def block_scale(own_key, dims, pieces, least, largest):
    level = 1.0
    for position, blocks in pieces:
        draws = jax.random.uniform(jax.random.fold_in(jax.random.fold_in(own_key, 6), position), (blocks,), jnp.float32, least / len(pieces), largest / len(pieces))
        level = level * jnp.repeat(jnp.exp(draws), dims[position] // blocks).reshape((-1,) + (1,) * (len(dims) - 1 - position))
    return level


def noise(rng, dims, spread, most, pieces=(), kind=jnp.bfloat16):
    gain = block_scale(rng, dims, pieces, -0.22, 0.18) if pieces else 1.0
    entries = jax.random.normal(rng, dims, jnp.float32) * spread * gain
    return jnp.minimum(jnp.maximum(entries, -most), most).astype(kind)


def setup_inputs(seed: int = 0) -> dict:
    key_of = jax.random.split(jax.random.key(seed), 7)
    return {
        "wind_east": noise(key_of[0], (LAT, LEVELS, LON), 1.0, 6.0, ((0, 32), (1, 16)), jnp.float32),
        "wind_north": noise(key_of[1], (LAT, LEVELS, LON), 1.0, 6.0, ((0, 32), (1, 16)), jnp.float32),
        "pot_temp": jnp.clip(jnp.exp(math.log(2.0) - 1.3862944 * jax.random.uniform(key_of[2], (LAT, LEVELS, LON), jnp.float32) ** block_scale(key_of[2], (LAT, LEVELS, LON), ((0, 32), (1, 16)), -0.2, 0.2)), 0.5, 2.0),
        "thickness": jnp.clip(0.5 + 1.0 * jax.random.uniform(key_of[3], (LAT, LEVELS, LON), jnp.float32) ** block_scale(key_of[3], (LAT, LEVELS, LON), ((0, 32), (1, 16)), -0.2, 0.2), 0.5, 1.5),
        "source_level": draw_source_level(jax.random.fold_in(key_of[6], 71), 0),
        "fraction": jnp.clip(1.0 * jax.random.uniform(key_of[5], (LAT, LEVELS, LON), jnp.float32) ** block_scale(key_of[5], (LAT, LEVELS, LON), ((0, 32), (1, 16)), -0.2, 0.2), 0.0, 1.0),
    }


def to_east(field):
    return jnp.roll(field, -1, axis=-1)

def to_west(field):
    return jnp.roll(field, 1, axis=-1)

def from_north(field):
    return jnp.concatenate([field[1:], jnp.zeros_like(field[:1])], axis=0)

def from_south(field):
    return jnp.concatenate([jnp.zeros_like(field[:1]), field[:-1]], axis=0)

def upwind_flux(speed, behind, ahead):
    return jnp.maximum(speed, 0.0) * behind + jnp.minimum(speed, 0.0) * ahead

def coriolis_of(row_index, lat_total):
    angle = math.pi * ((row_index.astype(jnp.float32) + 0.5) / lat_total - 0.5)
    return (0.15 * jnp.sin(angle))[:, None, None]

def load_suffix(temp_field, thick_field):
    column_load = thick_field * temp_field
    suffix_load = jnp.flip(jnp.cumsum(jnp.flip(column_load, 1), axis=1), 1)
    return (column_load, suffix_load)

def advance(east_wind, north_wind, temp_field, thick_field, geopot, northern, southern, coriolis):
    wind_n, thick_n, temp_n, geo_n = northern
    wind_s, thick_s, temp_s, geo_s = southern
    new_east = east_wind - 0.05 * (to_east(geopot) - to_west(geopot)) + coriolis * north_wind
    new_north = north_wind - 0.05 * (geo_n - geo_s) - coriolis * east_wind
    flux_x = upwind_flux(0.5 * (east_wind + to_east(east_wind)), thick_field, to_east(thick_field))
    flux_up = upwind_flux(0.5 * (north_wind + wind_n), thick_field, thick_n)
    flux_down = upwind_flux(0.5 * (wind_s + north_wind), thick_s, thick_field)
    new_thick = thick_field - 0.1 * (flux_x - to_west(flux_x) + flux_up - flux_down)
    new_temp = temp_field - 0.05 * (east_wind * (to_east(temp_field) - to_west(temp_field)) + north_wind * (temp_n - temp_s))
    return (new_east, new_north, new_temp, new_thick)

def reference(wind_east, wind_north, pot_temp, thickness, source_level, fraction):
    height_scale = 1.0 / math.sqrt(LEVELS)
    coriolis = coriolis_of(jnp.arange(LAT, dtype=jnp.int32), LAT)
    east_wind, north_wind, temp_field, thick_field = (wind_east, wind_north, pot_temp, thickness)
    for substep in range(STEPS):
        column_load, suffix_load = load_suffix(temp_field, thick_field)
        geopot = (suffix_load - 0.5 * column_load) * height_scale
        stacked = (north_wind, thick_field, temp_field, geopot)
        northern = tuple((from_north(member) for member in stacked))
        southern = tuple((from_south(member) for member in stacked))
        east_wind, north_wind, temp_field, thick_field = advance(east_wind, north_wind, temp_field, thick_field, geopot, northern, southern, coriolis)
    contents = []
    for member in (east_wind * thick_field, north_wind * thick_field, temp_field * thick_field, thick_field):
        prefix = jnp.cumsum(member, axis=1) - member
        mass_at = jnp.take_along_axis(prefix, source_level, axis=1) + fraction * jnp.take_along_axis(member, source_level, axis=1)
        mass_prior = jnp.concatenate([jnp.zeros_like(mass_at[:, :1]), mass_at[:, :-1]], axis=1)
        contents.append(mass_at - mass_prior)
    return (contents[0], contents[1], contents[2], contents[3])
```

```python
import functools
import math

import jax
import jax.numpy as jnp
from jax import lax
from jax.experimental import pallas as pl
from jax.experimental.pallas import tpu as pltpu
from jax.sharding import PartitionSpec as P

STEPS = 4
LANES = 128
BLOCK = 8


def send_kernel(u_ref, v_ref, t_ref, d_ref, f_ref, s_ref, state_ref, target_ref, wide, narrow):
    lon = u_ref.shape[-1]
    count, width, _ = state_ref.shape
    chunk = lon // count
    half = chunk // 2
    rim = (width - chunk) // 2
    levels = s_ref[...].astype(jnp.float32)
    for at in range(0, lon, LANES):
        cols = slice(at, at + LANES)
        block = jnp.concatenate(
            [ref[:, :, cols].reshape(-1, LANES) for ref in (u_ref, v_ref, t_ref, d_ref)], axis=0
        )
        wide[BLOCK + at : BLOCK + at + LANES, :] = block.T
        pair = [f_ref[:, :, cols].reshape(-1, LANES), levels[:, :, cols].reshape(-1, LANES)]
        narrow[at : at + LANES, :] = jnp.concatenate(pair + pair, axis=0).T
    wide[:BLOCK, :] = wide[lon : lon + BLOCK, :]
    wide[lon + BLOCK :, :] = wide[BLOCK : 2 * BLOCK, :]
    narrow[lon:, :] = jnp.zeros((narrow.shape[0] - lon, LANES), jnp.float32)
    rows = target_ref.shape[1]
    first = lax.broadcasted_iota(jnp.int32, (rows, LANES), 1) < LANES // 2
    for c in range(count):
        at = BLOCK + c * chunk - rim
        state_ref[c] = wide[at : at + width, :]
        at = c * chunk
        target_ref[c] = jnp.where(
            first, narrow[at : at + rows, :], narrow[at + half : at + half + rows, :]
        )


def swap_blocks(tiles):
    lane = lax.broadcasted_iota(jnp.int32, tiles[0].shape, 1) // BLOCK
    count = len(tiles)
    tiles = list(tiles)
    bit = 1
    while bit < count:
        upper = (lane & bit) != 0
        for low in range(count):
            if low & bit:
                continue
            high = low | bit
            a, b = tiles[low], tiles[high]
            tiles[low] = jnp.where(upper, pltpu.roll(b, bit * BLOCK, 1), a)
            tiles[high] = jnp.where(upper, b, pltpu.roll(a, LANES - bit * BLOCK, 1))
        bit *= 2
    return tiles


def split3(x):
    hi = x.astype(jnp.bfloat16)
    rest = x - hi.astype(jnp.float32)
    mid = rest.astype(jnp.bfloat16)
    low = (rest - mid.astype(jnp.float32)).astype(jnp.bfloat16)
    return hi, mid, low


def times_exact(x, matrix):
    return sum(jnp.dot(part, matrix, preferred_element_type=jnp.float32) for part in split3(x))


def core_kernel(own_ref, north_ref, south_ref, target_ref, out_ref, *scratch):
    state = (scratch[0:4], scratch[4:8])
    geo, place, result = scratch[8:11]
    count, width, _ = own_ref.shape
    chunk = out_ref.shape[1]
    half = chunk // 2
    rim = (width - chunk) // 2
    lat = lax.axis_index("lat")
    lat_total = lax.axis_size("lat") * 4
    rows = 12

    def unpack(i, carry):
        at = pl.ds(pl.multiple_of(i * BLOCK, BLOCK), BLOCK)
        for ref, base in ((south_ref, 0), (own_ref, 4), (north_ref, 8)):
            tiles = swap_blocks([ref[s, at, :] for s in range(count)])
            for f in range(4):
                for r in range(4):
                    state[0][f][base + r, at, :] = tiles[4 * f + r]
        return carry

    lax.fori_loop(0, width // BLOCK, unpack, 0)

    for i in range(target_ref.shape[1] // BLOCK):
        at = pl.ds(i * BLOCK, BLOCK)
        tiles = swap_blocks([target_ref[s, at, :] for s in range(count)])
        for j in range(2):
            keep = min(BLOCK, half - i * BLOCK)
            for k in range(8):
                place[k, j * half + i * BLOCK : j * half + i * BLOCK + keep, :] = tiles[8 * j + k][:keep]

    row_level = lax.broadcasted_iota(jnp.int32, (LANES, LANES), 0)
    col_level = lax.broadcasted_iota(jnp.int32, (LANES, LANES), 1)
    below = jnp.where(row_level > col_level, 1.0, jnp.where(row_level == col_level, 0.5, 0.0))
    below = below.astype(jnp.bfloat16)
    above = jnp.where(row_level < col_level, 1.0, 0.0).astype(jnp.bfloat16)
    slope = 0.05 / math.sqrt(LANES)

    row_index = lax.broadcasted_iota(jnp.int32, (16, LANES), 0) + (lat * 4 - 4)
    angle = math.pi * ((row_index.astype(jnp.float32) + 0.5) / lat_total - 0.5)
    result[0, :16, :] = 0.15 * jnp.sin(angle)

    def east(x):
        return pltpu.roll(x, width - 1, 0)

    def west(x):
        return pltpu.roll(x, 1, 0)

    def upwind(speed, behind, ahead):
        return jnp.maximum(speed, 0.0) * behind + jnp.minimum(speed, 0.0) * ahead

    for step in range(STEPS):
        u_ref, v_ref, t_ref, d_ref = state[step % 2]
        new = state[1 - step % 2]

        def potential(j, carry):
            geo[j] = times_exact(d_ref[j] * t_ref[j], below)
            return carry

        lax.fori_loop(step, rows - step, potential, 0)

        def advance(j, flux_down):
            u, v, t, d = u_ref[j], v_ref[j], t_ref[j], d_ref[j]
            v_n, d_n = v_ref[j + 1], d_ref[j + 1]
            g = geo[j]
            cor = result[0, pl.ds(j, 1), :]
            inside = jnp.logical_and(lat * 4 - 4 + j >= 0, lat * 4 - 4 + j < lat_total)
            d_e = east(d)
            flux_x = upwind(0.5 * (u + east(u)), d, d_e)
            flux_up = upwind(0.5 * (v + v_n), d, d_n)
            new_u = u - slope * (east(g) - west(g)) + cor * v
            new_v = v - slope * (geo[j + 1] - geo[j - 1]) - cor * u
            new_d = d - 0.1 * (flux_x - west(flux_x) + flux_up - flux_down)
            new_t = t - 0.05 * (u * (east(t) - west(t)) + v * (t_ref[j + 1] - t_ref[j - 1]))
            for ref, value in zip(new, (new_u, new_v, new_t, new_d)):
                ref[j] = jnp.where(inside, value, 0.0)
            return flux_up

        first = step + 1
        flux_start = upwind(0.5 * (v_ref[step] + v_ref[first]), d_ref[step], d_ref[first])
        lax.fori_loop(first, rows - first, advance, flux_start)

    final = state[STEPS % 2]
    lane = lax.broadcasted_iota(jnp.int32, (chunk, LANES), 1)

    def remap(r, carry):
        source = place[4 + r].astype(jnp.int32)
        part = place[r]
        mid = pl.ds(rim, chunk)
        u, v, t, d = (ref[4 + r, mid, :] for ref in final)
        for f, q in enumerate((u * d, v * d, t * d, d)):
            prefix = times_exact(q, above)
            mass = jnp.take_along_axis(prefix, source, axis=1) + part * jnp.take_along_axis(
                q, source, axis=1
            )
            result[4 * f + r] = mass - jnp.where(lane == 0, 0.0, pltpu.roll(mass, 1, 1))
        return carry

    lax.fori_loop(0, 4, remap, 0)

    def pack(i, carry):
        at = pl.ds(pl.multiple_of(i * BLOCK, BLOCK), BLOCK)
        for s, tile in enumerate(swap_blocks([result[k, at, :] for k in range(count)])):
            out_ref[s, at, :] = tile
        return carry

    lax.fori_loop(0, chunk // BLOCK, pack, 0)


def receive_kernel(in_ref, *out_refs):
    lon = out_refs[0].shape[-1]
    flat = in_ref[...].reshape(lon, LANES)
    for at in range(0, lon, LANES):
        block = flat[at : at + LANES, :].T
        for f, ref in enumerate(out_refs):
            ref[:, :, at : at + LANES] = block[32 * f : 32 * f + 32].reshape(4, 8, LANES)


def whole(count):
    return [pl.BlockSpec(memory_space=pltpu.VMEM)] * count


def call(kernel, shapes, scratch, *args):
    out_shape = [jax.ShapeDtypeStruct(shape, jnp.float32) for shape in shapes]
    return pl.pallas_call(
        kernel,
        out_shape=out_shape,
        in_specs=whole(len(args)),
        out_specs=whole(len(out_shape)),
        scratch_shapes=[pltpu.VMEM(shape, jnp.float32) for shape in scratch],
        compiler_params=pltpu.CompilerParams(vmem_limit_bytes=40 * 2**20),
    )(*args)


def body(wind_east, wind_north, pot_temp, thickness, source_level, fraction):
    lon = wind_east.shape[-1]
    count = lax.axis_size("lev")
    blocks = lax.axis_size("lat")
    chunk = lon // count
    width = chunk + 2 * STEPS
    narrow = -(-(chunk // 2) // BLOCK) * BLOCK
    state, target = call(
        send_kernel,
        [(count, width, LANES), (count, narrow, LANES)],
        [(lon + 2 * BLOCK, LANES), (lon + BLOCK, LANES)],
        wind_east, wind_north, pot_temp, thickness, fraction, source_level,
    )
    own = lax.all_to_all(state, "lev", 0, 0, tiled=True)
    north = lax.ppermute(own, "lat", [(i + 1, i) for i in range(blocks - 1)])
    south = lax.ppermute(own, "lat", [(i, i + 1) for i in range(blocks - 1)])
    own, target = lax.optimization_barrier((own, target))
    target = lax.all_to_all(target, "lev", 0, 0, tiled=True)
    field = (12, width, LANES)
    (contents,) = call(
        core_kernel,
        [(count, chunk, LANES)],
        [field] * 9 + [(8, chunk, LANES), (16, chunk, LANES)],
        own, north, south, target,
    )
    contents = lax.all_to_all(contents, "lev", 0, 0, tiled=True)
    return tuple(call(receive_kernel, [wind_east.shape] * 4, [], contents))


def solution(mesh):
    placed = P("lat", "lev", None)
    return jax.shard_map(
        body, mesh=mesh, in_specs=(placed,) * 6, out_specs=(placed,) * 4, check_vma=False
    )
```

```python
import math

import jax
import jax.numpy as jnp
from jax import lax
from jax.experimental import pallas as pl
from jax.experimental.pallas import tpu as pltpu
from jax.sharding import PartitionSpec as P

STEPS = 4
LANES = 128
BLOCK = 8


def send_kernel(u_in, v_in, t_in, d_in, f_in, s_in, state_out, target_out, *scratch):
    fields, levels = scratch[:5], scratch[5]
    wide_stack, narrow_stack, wide, narrow, state_ref, target_ref, sems = scratch[6:]
    rows, _, lon = u_in.shape
    count, width, _ = state_ref.shape
    chunk = lon // count
    half = chunk // 2
    rim = (width - chunk) // 2
    mine = lax.axis_index("lev")
    copies = [
        pltpu.make_async_copy(source, target, sems.at[i])
        for i, (source, target) in enumerate(
            zip((u_in, v_in, t_in, d_in, f_in, s_in), fields + (levels,))
        )
    ]
    for copy in copies:
        copy.start()

    def block(j):
        return lax.rem(mine + j, count)

    for f in range(4):
        copies[f].wait()
        for r in range(rows):
            wide_stack[block(rows * f + r)] = fields[f][r]
    for at in range(0, lon, LANES):
        wide[BLOCK + at : BLOCK + at + LANES, :] = (
            wide_stack[:, :, at : at + LANES].reshape(LANES, LANES).T
        )
    wide[:BLOCK, :] = wide[lon : lon + BLOCK, :]
    wide[lon + BLOCK :, :] = wide[BLOCK : 2 * BLOCK, :]
    for c in range(count):
        at = BLOCK + c * chunk - rim
        state_ref[c] = wide[at : at + width, :]
    out = [pltpu.make_async_copy(state_ref, state_out, sems.at[0])]
    out[0].start()

    copies[4].wait()
    copies[5].wait()
    for h in range(2):
        for r in range(rows):
            narrow_stack[block(8 * h + r)] = fields[4][r]
            narrow_stack[block(8 * h + 4 + r)] = levels[r].astype(jnp.float32)
    for at in range(0, lon, LANES):
        narrow[at : at + LANES, :] = narrow_stack[:, :, at : at + LANES].reshape(LANES, LANES).T
    narrow[lon:, :] = jnp.zeros((narrow.shape[0] - lon, LANES), jnp.float32)
    size = target_ref.shape[1]
    place = lax.broadcasted_iota(jnp.int32, (size, LANES), 1) // BLOCK
    first = lax.rem(place - mine + count, count) < count // 2
    for c in range(count):
        at = c * chunk
        target_ref[c] = jnp.where(
            first, narrow[at : at + size, :], narrow[at + half : at + half + size, :]
        )
    out.append(pltpu.make_async_copy(target_ref, target_out, sems.at[1]))
    out[1].start()
    for copy in out:
        copy.wait()


def spread(tiles):
    count = len(tiles)
    lane = lax.broadcasted_iota(jnp.int32, tiles[0].shape, 1) // BLOCK
    tiles = [tiles[(count - t) % count] for t in range(count)]
    bit = 1
    while bit < count:
        upper = (lane & bit) != 0
        tiles = [jnp.where(upper, tiles[t - bit], tiles[t]) for t in range(count)]
        bit *= 2
    return tiles


def gathered(tiles):
    return [
        z if t == 0 else pltpu.roll(z, LANES - BLOCK * t, 1) for t, z in enumerate(spread(tiles))
    ]


def scattered(tiles):
    return spread([x if t == 0 else pltpu.roll(x, BLOCK * t, 1) for t, x in enumerate(tiles)])


def times_exact(x, matrix, parts):
    total = None
    for part in range(parts):
        piece = x.astype(jnp.bfloat16)
        term = jnp.dot(piece, matrix, preferred_element_type=jnp.float32)
        total = term if total is None else total + term
        if part < parts - 1:
            x = x - piece.astype(jnp.float32)
    return total


def core_kernel(own_ref, north_ref, south_ref, target_ref, contents_out, *scratch):
    state = (scratch[0:4], scratch[4:8])
    geo, place, result, spin, out_ref, sem = scratch[8:14]
    count, width, _ = own_ref.shape
    chunk = out_ref.shape[1]
    half = chunk // 2
    rim = (width - chunk) // 2
    lat = lax.axis_index("lat")
    lat_rows = lax.axis_size("lat") * 4
    rows = 12

    for i in range(target_ref.shape[1] // BLOCK):
        at = pl.ds(i * BLOCK, BLOCK)
        tiles = gathered([target_ref[s, at, :] for s in range(count)])
        keep = min(BLOCK, half - i * BLOCK)
        for j in range(2):
            for k in range(8):
                start = j * half + i * BLOCK
                place[k, start : start + keep, :] = tiles[8 * j + k][:keep]

    def unpack(i, carry):
        at = pl.ds(pl.multiple_of(i * BLOCK, BLOCK), BLOCK)
        for ref, base in ((south_ref, 0), (own_ref, 4), (north_ref, 8)):
            tiles = gathered([ref[s, at, :] for s in range(count)])
            for f in range(4):
                for r in range(4):
                    state[0][f][base + r, at, :] = tiles[4 * f + r]
        return carry

    lax.fori_loop(0, width // BLOCK, unpack, 0, unroll=2)

    row_level = lax.broadcasted_iota(jnp.int32, (LANES, LANES), 0)
    col_level = lax.broadcasted_iota(jnp.int32, (LANES, LANES), 1)
    below = jnp.where(row_level > col_level, 1.0, jnp.where(row_level == col_level, 0.5, 0.0))
    below = below.astype(jnp.bfloat16)
    above = jnp.where(row_level < col_level, 1.0, 0.0).astype(jnp.bfloat16)
    slope = 0.05 / math.sqrt(LANES)

    row_index = lax.broadcasted_iota(jnp.int32, (16, LANES), 0) + (lat * 4 - 4)
    angle = math.pi * ((row_index.astype(jnp.float32) + 0.5) / lat_rows - 0.5)
    spin[...] = 0.15 * jnp.sin(angle)

    def east(x):
        return pltpu.roll(x, width - 1, 0)

    def west(x):
        return pltpu.roll(x, 1, 0)

    def upwind(speed, behind, ahead):
        return speed * jnp.where(speed > 0.0, behind, ahead)

    for step in range(STEPS):
        u_ref, v_ref, t_ref, d_ref = state[step % 2]
        new = state[1 - step % 2]
        size = rows - 2 * step
        load = d_ref[step : rows - step] * t_ref[step : rows - step]
        heights = slope * times_exact(load.reshape(size * width, LANES), below, 3)
        geo[step : rows - step] = heights.reshape(size, width, LANES)

        def advance(j, flux_down):
            u, v, t, d = u_ref[j], v_ref[j], t_ref[j], d_ref[j]
            v_n, d_n = v_ref[j + 1], d_ref[j + 1]
            g = geo[j]
            cor = spin[pl.ds(j, 1), :]
            flux_x = upwind(u + east(u), d, east(d))
            flux_up = upwind(v + v_n, d, d_n)
            new[0][j] = u - (east(g) - west(g)) + cor * v
            new[1][j] = v - (geo[j + 1] - geo[j - 1]) - cor * u
            new[2][j] = t - 0.05 * (
                u * (east(t) - west(t)) + v * (t_ref[j + 1] - t_ref[j - 1])
            )
            new[3][j] = d - 0.05 * (flux_x - west(flux_x) + flux_up - flux_down)
            return flux_up

        first = step + 1
        flux_start = upwind(v_ref[step] + v_ref[first], d_ref[step], d_ref[first])
        lax.fori_loop(first, rows - first, advance, flux_start, unroll=2)

        if first < 4:

            @pl.when(lat == 0)
            def _():
                for ref in new[1:]:
                    ref[:4] = jnp.zeros((4, width, LANES), jnp.float32)

            @pl.when(lat == lax.axis_size("lat") - 1)
            def _():
                for ref in new[1:]:
                    ref[8:] = jnp.zeros((4, width, LANES), jnp.float32)

    u, v, t, d = (ref[4:8, rim : rim + chunk, :] for ref in state[STEPS % 2])
    for f, q in enumerate((u * d, v * d, t * d, d)):
        result[4 * f : 4 * f + 4] = q
    flat = result[...].reshape(count * chunk, LANES)
    geo_rows = times_exact(flat, above, 3).reshape(count, chunk, LANES)
    lane = lax.broadcasted_iota(jnp.int32, (chunk, LANES), 1)
    for r in range(4):
        source = place[4 + r].astype(jnp.int32)
        part = place[r]
        for f in range(4):
            k = 4 * f + r
            mass = jnp.take_along_axis(geo_rows[k], source, axis=1) + part * jnp.take_along_axis(
                result[k], source, axis=1
            )
            result[k] = mass - jnp.where(lane == 0, 0.0, pltpu.roll(mass, 1, 1))

    def pack(i, carry):
        at = pl.ds(pl.multiple_of(i * BLOCK, BLOCK), BLOCK)
        for s, tile in enumerate(scattered([result[k, at, :] for k in range(count)])):
            out_ref[s, at, :] = tile
        return carry

    lax.fori_loop(0, chunk // BLOCK, pack, 0, unroll=3)
    copy = pltpu.make_async_copy(out_ref, contents_out, sem)
    copy.start()
    copy.wait()


def receive_kernel(in_ref, *refs):
    outs, turned = refs[:4], refs[4]
    rows, _, lon = outs[0].shape
    count = in_ref.shape[0]
    mine = lax.axis_index("lev")
    flat = in_ref[...].reshape(lon, LANES)
    for at in range(0, lon, LANES):
        turned[:, :, at : at + LANES] = flat[at : at + LANES, :].T.reshape(count, BLOCK, LANES)
    for f, ref in enumerate(outs):
        for r in range(rows):
            ref[r] = turned[lax.rem(mine + rows * f + r, count)]


def call(kernel, ins, outs, scratch, *args):
    shapes = [jax.ShapeDtypeStruct(shape, jnp.float32) for shape, _ in outs]
    return pl.pallas_call(
        kernel,
        out_shape=shapes,
        in_specs=[pl.BlockSpec(memory_space=ins)] * len(args),
        out_specs=[pl.BlockSpec(memory_space=space) for _, space in outs],
        scratch_shapes=[
            pltpu.VMEM(shape, jnp.float32) if isinstance(shape, tuple) else shape
            for shape in scratch
        ],
        compiler_params=pltpu.CompilerParams(vmem_limit_bytes=40 * 2**20),
    )(*args)


def body(wind_east, wind_north, pot_temp, thickness, source_level, fraction):
    rows, depth, lon = wind_east.shape
    count = lax.axis_size("lev")
    blocks = lax.axis_size("lat")
    chunk = lon // count
    width = chunk + 2 * STEPS
    size = -(-(chunk // 2) // BLOCK) * BLOCK
    slab = wind_east.shape
    stack = (count, depth, lon)
    state, target = call(
        send_kernel,
        pltpu.HBM,
        [((count, width, LANES), pltpu.HBM), ((count, size, LANES), pltpu.HBM)],
        [slab] * 5
        + [pltpu.VMEM(slab, jnp.int32)]
        + [stack, stack, (lon + 2 * BLOCK, LANES), (lon + BLOCK, LANES)]
        + [(count, width, LANES), (count, size, LANES), pltpu.SemaphoreType.DMA((6,))],
        wind_east, wind_north, pot_temp, thickness, fraction, source_level,
    )
    own = lax.all_to_all(state, "lev", 0, 0, tiled=True)
    north = lax.ppermute(own, "lat", [(i + 1, i) for i in range(blocks - 1)])
    south = lax.ppermute(own, "lat", [(i, i + 1) for i in range(blocks - 1)])
    own, target = lax.optimization_barrier((own, target))
    target = lax.all_to_all(target, "lev", 0, 0, tiled=True)
    (contents,) = call(
        core_kernel,
        pltpu.VMEM,
        [((count, chunk, LANES), pltpu.HBM)],
        [(3 * rows, width, LANES)] * 9
        + [(8, chunk, LANES), (count, chunk, LANES), (16, LANES), (count, chunk, LANES)]
        + [pltpu.SemaphoreType.DMA],
        own, north, south, target,
    )
    contents = lax.all_to_all(contents, "lev", 0, 0, tiled=True)
    return tuple(
        call(receive_kernel, pltpu.VMEM, [(slab, pltpu.VMEM)] * 4, [stack], contents)
    )


def solution(mesh):
    placed = P("lat", "lev", None)
    return jax.shard_map(
        body, mesh=mesh, in_specs=(placed,) * 6, out_specs=(placed,) * 4, check_vma=False
    )
```

```python
import math

import jax
import jax.numpy as jnp
from jax import lax
from jax.experimental import pallas as pl
from jax.experimental.pallas import tpu as pltpu
from jax.sharding import PartitionSpec as P

STEPS = 4
LANES = 128
BLOCK = 8


def fetch(sources, targets, sems):
    copies = [
        pltpu.make_async_copy(source, target, sems.at[i])
        for i, (source, target) in enumerate(zip(sources, targets))
    ]
    for copy in copies:
        copy.start()
    return copies


def turn(stack, flat, base):
    lon = stack.shape[-1]
    for at in range(0, lon, LANES):
        flat[base + at : base + at + LANES, :] = (
            stack[:, :, at : at + LANES].reshape(LANES, LANES).T
        )


def send_state(u_in, v_in, t_in, d_in, state_ref, *scratch):
    fields, (stack, flat, sems) = scratch[:4], scratch[4:]
    rows, _, lon = u_in.shape
    count, width, _ = state_ref.shape
    chunk = lon // count
    rim = (width - chunk) // 2
    mine = lax.axis_index("lev")
    copies = fetch((u_in, v_in, t_in, d_in), fields, sems)
    for f in range(4):
        copies[f].wait()
        for r in range(rows):
            stack[lax.rem(mine + rows * f + r, count)] = fields[f][r]
    turn(stack, flat, BLOCK)
    flat[:BLOCK, :] = flat[lon : lon + BLOCK, :]
    flat[lon + BLOCK :, :] = flat[BLOCK : 2 * BLOCK, :]
    for c in range(count):
        at = BLOCK + c * chunk - rim
        state_ref[c] = flat[at : at + width, :]


def send_target(f_in, s_in, target_ref, part, level, stack, flat, sems):
    rows, _, lon = f_in.shape
    count, size, _ = target_ref.shape
    chunk = lon // count
    half = chunk // 2
    mine = lax.axis_index("lev")
    for copy in fetch((f_in, s_in), (part, level), sems):
        copy.wait()
    for h in range(2):
        for r in range(rows):
            stack[lax.rem(mine + 8 * h + r, count)] = part[r]
            stack[lax.rem(mine + 8 * h + 4 + r, count)] = level[r].astype(jnp.float32)
    turn(stack, flat, 0)
    flat[lon:, :] = jnp.zeros((flat.shape[0] - lon, LANES), jnp.float32)
    place = lax.broadcasted_iota(jnp.int32, (size, LANES), 1) // BLOCK
    first = lax.rem(place - mine + count, count) < count // 2
    for c in range(count):
        at = c * chunk
        target_ref[c] = jnp.where(
            first, flat[at : at + size, :], flat[at + half : at + half + size, :]
        )


def spread(tiles):
    count = len(tiles)
    lane = lax.broadcasted_iota(jnp.int32, tiles[0].shape, 1) // BLOCK
    tiles = [tiles[(count - t) % count] for t in range(count)]
    bit = 1
    while bit < count:
        upper = (lane & bit) != 0
        tiles = [jnp.where(upper, tiles[t - bit], tiles[t]) for t in range(count)]
        bit *= 2
    return tiles


def gathered(tiles):
    return [
        z if t == 0 else pltpu.roll(z, LANES - BLOCK * t, 1) for t, z in enumerate(spread(tiles))
    ]


def scattered(tiles):
    return spread([x if t == 0 else pltpu.roll(x, BLOCK * t, 1) for t, x in enumerate(tiles)])


def times_exact(x, matrix, parts):
    total = None
    for part in range(parts):
        piece = x.astype(jnp.bfloat16)
        term = jnp.dot(piece, matrix, preferred_element_type=jnp.float32)
        total = term if total is None else total + term
        if part < parts - 1:
            x = x - piece.astype(jnp.float32)
    return total


def step_kernel(own_ref, north_ref, south_ref, contents_ref, prefix_ref, *scratch):
    state = (scratch[0:4], scratch[4:8])
    geo, spin = scratch[8:10]
    count, width, _ = own_ref.shape
    chunk = contents_ref.shape[1]
    rim = (width - chunk) // 2
    lat = lax.axis_index("lat")
    lat_rows = lax.axis_size("lat") * 4
    rows = 12

    def unpack(i, carry):
        at = pl.ds(pl.multiple_of(i * BLOCK, BLOCK), BLOCK)
        for ref, base in ((south_ref, 0), (own_ref, 4), (north_ref, 8)):
            tiles = gathered([ref[s, at, :] for s in range(count)])
            for f in range(4):
                for r in range(4):
                    state[0][f][base + r, at, :] = tiles[4 * f + r]
        return carry

    lax.fori_loop(0, width // BLOCK, unpack, 0, unroll=2)

    row_level = lax.broadcasted_iota(jnp.int32, (LANES, LANES), 0)
    col_level = lax.broadcasted_iota(jnp.int32, (LANES, LANES), 1)
    below = jnp.where(row_level > col_level, 1.0, jnp.where(row_level == col_level, 0.5, 0.0))
    below = below.astype(jnp.bfloat16)
    above = jnp.where(row_level < col_level, 1.0, 0.0).astype(jnp.bfloat16)
    slope = 0.05 / math.sqrt(LANES)

    row_index = lax.broadcasted_iota(jnp.int32, (16, LANES), 0) + (lat * 4 - 4)
    angle = math.pi * ((row_index.astype(jnp.float32) + 0.5) / lat_rows - 0.5)
    spin[...] = 0.15 * jnp.sin(angle)

    def east(x):
        return pltpu.roll(x, width - 1, 0)

    def west(x):
        return pltpu.roll(x, 1, 0)

    def upwind(speed, behind, ahead):
        return speed * jnp.where(speed > 0.0, behind, ahead)

    for step in range(STEPS):
        u_ref, v_ref, t_ref, d_ref = state[step % 2]
        new = state[1 - step % 2]
        size = rows - 2 * step
        load = d_ref[step : rows - step] * t_ref[step : rows - step]
        heights = slope * times_exact(load.reshape(size * width, LANES), below, 3)
        geo[step : rows - step] = heights.reshape(size, width, LANES)

        def advance(j, flux_down):
            u, v, t, d = u_ref[j], v_ref[j], t_ref[j], d_ref[j]
            v_n, d_n = v_ref[j + 1], d_ref[j + 1]
            g = geo[j]
            cor = spin[pl.ds(j, 1), :]
            flux_x = upwind(u + east(u), d, east(d))
            flux_up = upwind(v + v_n, d, d_n)
            new[0][j] = u - (east(g) - west(g)) + cor * v
            new[1][j] = v - (geo[j + 1] - geo[j - 1]) - cor * u
            new[2][j] = t - 0.05 * (
                u * (east(t) - west(t)) + v * (t_ref[j + 1] - t_ref[j - 1])
            )
            new[3][j] = d - 0.05 * (flux_x - west(flux_x) + flux_up - flux_down)
            return flux_up

        first = step + 1
        flux_start = upwind(v_ref[step] + v_ref[first], d_ref[step], d_ref[first])
        lax.fori_loop(first, rows - first, advance, flux_start, unroll=2)

        if first < 4:

            @pl.when(lat == 0)
            def _():
                for ref in new[1:]:
                    ref[:4] = jnp.zeros((4, width, LANES), jnp.float32)

            @pl.when(lat == lax.axis_size("lat") - 1)
            def _():
                for ref in new[1:]:
                    ref[8:] = jnp.zeros((4, width, LANES), jnp.float32)

    u, v, t, d = (ref[4:8, rim : rim + chunk, :] for ref in state[STEPS % 2])
    for f, q in enumerate((u * d, v * d, t * d, d)):
        contents_ref[4 * f : 4 * f + 4] = q
    flat = contents_ref[...].reshape(count * chunk, LANES)
    prefix_ref[...] = times_exact(flat, above, 3).reshape(count, chunk, LANES)


def remap_kernel(target_ref, contents_ref, prefix_ref, out_ref, place, result):
    count, chunk, _ = contents_ref.shape
    half = chunk // 2
    for i in range(target_ref.shape[1] // BLOCK):
        at = pl.ds(i * BLOCK, BLOCK)
        tiles = gathered([target_ref[s, at, :] for s in range(count)])
        keep = min(BLOCK, half - i * BLOCK)
        for j in range(2):
            for k in range(8):
                start = j * half + i * BLOCK
                place[k, start : start + keep, :] = tiles[8 * j + k][:keep]
    lane = lax.broadcasted_iota(jnp.int32, (chunk, LANES), 1)
    for r in range(4):
        source = place[4 + r].astype(jnp.int32)
        part = place[r]
        for f in range(4):
            k = 4 * f + r
            mass = jnp.take_along_axis(
                prefix_ref[k], source, axis=1
            ) + part * jnp.take_along_axis(contents_ref[k], source, axis=1)
            result[k] = mass - jnp.where(lane == 0, 0.0, pltpu.roll(mass, 1, 1))

    def pack(i, carry):
        at = pl.ds(pl.multiple_of(i * BLOCK, BLOCK), BLOCK)
        for s, tile in enumerate(scattered([result[k, at, :] for k in range(count)])):
            out_ref[s, at, :] = tile
        return carry

    lax.fori_loop(0, chunk // BLOCK, pack, 0, unroll=3)


def receive_kernel(in_ref, *refs):
    outs, turned = refs[:4], refs[4]
    rows, _, lon = outs[0].shape
    count = in_ref.shape[0]
    mine = lax.axis_index("lev")
    flat = in_ref[...].reshape(lon, LANES)
    for at in range(0, lon, LANES):
        turned[:, :, at : at + LANES] = flat[at : at + LANES, :].T.reshape(count, BLOCK, LANES)
    for f, ref in enumerate(outs):
        for r in range(rows):
            ref[r] = turned[lax.rem(mine + rows * f + r, count)]


def call(kernel, ins, outs, scratch, *args, limit=40 * 2**20, flops=0):
    shapes = [jax.ShapeDtypeStruct(shape, jnp.float32) for shape in outs]
    moved = sum(4 * math.prod(a.shape) for a in (*args, *shapes))
    return pl.pallas_call(
        kernel,
        out_shape=shapes,
        in_specs=[pl.BlockSpec(memory_space=ins)] * len(args),
        out_specs=[pl.BlockSpec(memory_space=pltpu.VMEM)] * len(outs),
        scratch_shapes=[
            pltpu.VMEM(shape, jnp.float32) if isinstance(shape, tuple) else shape
            for shape in scratch
        ],
        cost_estimate=pl.CostEstimate(flops=flops, bytes_accessed=moved, transcendentals=0),
        compiler_params=pltpu.CompilerParams(vmem_limit_bytes=limit),
    )(*args)


def body(wind_east, wind_north, pot_temp, thickness, source_level, fraction):
    rows, depth, lon = wind_east.shape
    count = lax.axis_size("lev")
    blocks = lax.axis_size("lat")
    chunk = lon // count
    width = chunk + 2 * STEPS
    size = -(-(chunk // 2) // BLOCK) * BLOCK
    slab = wind_east.shape
    stack = (count, depth, lon)
    column = (count, chunk, LANES)
    (state,) = call(
        send_state, pltpu.HBM, [(count, width, LANES)],
        [slab] * 4 + [stack, (lon + 2 * BLOCK, LANES), pltpu.SemaphoreType.DMA((4,))],
        wind_east, wind_north, pot_temp, thickness, limit=60 * 2**20,
    )
    (target,) = call(
        send_target, pltpu.HBM, [(count, size, LANES)],
        [slab, pltpu.VMEM(slab, jnp.int32), stack, (lon + BLOCK, LANES)]
        + [pltpu.SemaphoreType.DMA((2,))],
        fraction, source_level, limit=60 * 2**20,
    )
    own = lax.all_to_all(state, "lev", 0, 0, tiled=True)
    own, target = lax.optimization_barrier((own, target))
    north = lax.ppermute(own, "lat", [(i + 1, i) for i in range(blocks - 1)])
    south = lax.ppermute(own, "lat", [(i, i + 1) for i in range(blocks - 1)])
    target = lax.all_to_all(target, "lev", 0, 0, tiled=True)
    contents, prefix = call(
        step_kernel, pltpu.VMEM, [column] * 2,
        [(3 * rows, width, LANES)] * 9 + [(16, LANES)],
        own, north, south, flops=3 * 10**8,
    )
    (contents,) = call(
        remap_kernel, pltpu.VMEM, [column], [(8, chunk, LANES), column],
        target, contents, prefix,
    )
    contents = lax.all_to_all(contents, "lev", 0, 0, tiled=True)
    return tuple(call(receive_kernel, pltpu.VMEM, [slab] * 4, [stack], contents))


def solution(mesh):
    placed = P("lat", "lev", None)
    return jax.shard_map(
        body, mesh=mesh, in_specs=(placed,) * 6, out_specs=(placed,) * 4, check_vma=False
    )
```

```python
import math

import jax
import jax.numpy as jnp
from jax import lax
from jax.experimental import pallas as pl
from jax.experimental.pallas import tpu as pltpu
from jax.sharding import PartitionSpec as P

STEPS = 4
LANES = 128
BLOCK = 8


def slot(chunk):
    half = lax.axis_size("lat") // 2
    return chunk + lax.div(lax.axis_index("lat"), half) * (1 - 2 * (chunk % 2))


def fetch(sources, targets, sems):
    copies = [
        pltpu.make_async_copy(source, target, sems.at[i])
        for i, (source, target) in enumerate(zip(sources, targets))
    ]
    for copy in copies:
        copy.start()
    return copies


def turn(stack, flat, base):
    lon = stack.shape[-1]
    for at in range(0, lon, LANES):
        flat[base + at : base + at + LANES, :] = (
            stack[:, :, at : at + LANES].reshape(LANES, LANES).T
        )


def send_state(u_in, v_in, t_in, d_in, state_out, stack, flat, in_sems, out_sems):
    rows, _, lon = u_in.shape
    count, width, _ = state_out.shape
    chunk = lon // count
    rim = (width - chunk) // 2
    mine = lax.axis_index("lev")
    places = [stack.at[lax.rem(mine + j, count)] for j in range(4 * rows)]
    sources = [ref.at[r] for ref in (u_in, v_in, t_in, d_in) for r in range(rows)]
    for copy in fetch(sources, places, in_sems):
        copy.wait()

    base = BLOCK + rim
    outs = [
        pltpu.make_async_copy(
            flat.at[pl.ds(BLOCK + c * chunk, width)], state_out.at[slot(c)], out_sems.at[c]
        )
        for c in range(count)
    ]
    sent = 1
    for at in range(0, lon, LANES):
        flat[base + at : base + at + LANES, :] = (
            stack[:, :, at : at + LANES].reshape(LANES, LANES).T
        )
        while sent < count - 1 and (sent + 1) * chunk + rim <= at + LANES:
            outs[sent].start()
            sent += 1
    flat[base - rim : base, :] = flat[base + lon - rim : base + lon, :]
    flat[base + lon :, :] = flat[base : base + rim, :]
    outs[0].start()
    for c in range(sent, count):
        outs[c].start()
    for copy in outs:
        copy.wait()


def send_target(f_in, s_in, target_ref, part, level, stack, flat, sems):
    rows, _, lon = f_in.shape
    count, size, _ = target_ref.shape
    chunk = lon // count
    half = chunk // 2
    mine = lax.axis_index("lev")
    for copy in fetch((f_in, s_in), (part, level), sems):
        copy.wait()
    for h in range(2):
        for r in range(rows):
            stack[lax.rem(mine + 8 * h + r, count)] = part[r]
            stack[lax.rem(mine + 8 * h + 4 + r, count)] = level[r].astype(jnp.float32)
    turn(stack, flat, 0)
    flat[lon:, :] = jnp.zeros((flat.shape[0] - lon, LANES), jnp.float32)
    place = lax.broadcasted_iota(jnp.int32, (size, LANES), 1) // BLOCK
    first = lax.rem(place - mine + count, count) < count // 2
    for c in range(count):
        at = c * chunk
        target_ref[slot(c)] = jnp.where(
            first, flat[at : at + size, :], flat[at + half : at + half + size, :]
        )


def spread(tiles):
    count = len(tiles)
    lane = lax.broadcasted_iota(jnp.int32, tiles[0].shape, 1) // BLOCK
    tiles = [tiles[(count - t) % count] for t in range(count)]
    bit = 1
    while bit < count:
        upper = (lane & bit) != 0
        tiles = [jnp.where(upper, tiles[t - bit], tiles[t]) for t in range(count)]
        bit *= 2
    return tiles


def gathered(tiles):
    return [
        z if t == 0 else pltpu.roll(z, LANES - BLOCK * t, 1) for t, z in enumerate(spread(tiles))
    ]


def scattered(tiles):
    return spread([x if t == 0 else pltpu.roll(x, BLOCK * t, 1) for t, x in enumerate(tiles)])


def times_exact(x, matrix, parts):
    total = None
    for part in range(parts):
        piece = x.astype(jnp.bfloat16)
        term = jnp.dot(piece, matrix, preferred_element_type=jnp.float32)
        total = term if total is None else total + term
        if part < parts - 1:
            x = x - piece.astype(jnp.float32)
    return total


def unpack_state(raw_ref, out_ref):
    count, width, _ = raw_ref.shape
    for i in range(width // BLOCK):
        at = pl.ds(i * BLOCK, BLOCK)
        for k, tile in enumerate(gathered([raw_ref[s, at, :] for s in range(count)])):
            out_ref[k, at, :] = tile


def core_kernel(own_ref, near_ref, far_ref, place, out_ref, *scratch):
    buffers = (scratch[0:4], scratch[4:8])
    geo, spin, result = scratch[8:11]
    count, width, _ = own_ref.shape
    chunk = out_ref.shape[1]
    rim = (width - chunk) // 2
    lat = lax.axis_index("lat")
    lat_rows = lax.axis_size("lat") * 4
    rows = 12

    odd = lax.rem(lat, 2)
    for ref, base in ((far_ref, 8 * odd), (own_ref, 4), (near_ref, 8 - 8 * odd)):
        for f in range(4):
            buffers[0][f][pl.ds(base, 4)] = ref[4 * f : 4 * f + 4]

    def get(step, f, j):
        return buffers[step % 2][f][j]

    row_level = lax.broadcasted_iota(jnp.int32, (LANES, LANES), 0)
    col_level = lax.broadcasted_iota(jnp.int32, (LANES, LANES), 1)
    below = jnp.where(row_level > col_level, 1.0, jnp.where(row_level == col_level, 0.5, 0.0))
    below = below.astype(jnp.bfloat16)
    above = jnp.where(row_level < col_level, 1.0, 0.0).astype(jnp.bfloat16)
    slope = 0.05 / math.sqrt(LANES)

    row_index = lax.broadcasted_iota(jnp.int32, (16, LANES), 0) + (lat * 4 - 4)
    angle = math.pi * ((row_index.astype(jnp.float32) + 0.5) / lat_rows - 0.5)
    spin[...] = 0.15 * jnp.sin(angle)

    def east(x):
        return pltpu.roll(x, width - 1, 0)

    def west(x):
        return pltpu.roll(x, 1, 0)

    def upwind(speed, behind, ahead):
        return speed * jnp.where(speed > 0.0, behind, ahead)

    for step in range(STEPS):
        new = buffers[1 - step % 2]
        size = rows - 2 * step
        span = range(step, rows - step)
        load = jnp.concatenate([get(step, 3, j) * get(step, 2, j) for j in span], axis=0)
        heights = slope * times_exact(load, below, 3)
        geo[step : rows - step] = heights.reshape(size, width, LANES)
        flux_down = None
        for j in span:
            v, t, d = (get(step, f, j) for f in (1, 2, 3))
            if j == rows - step - 1:
                break
            v_n, t_n, d_n = (get(step, f, j + 1) for f in (1, 2, 3))
            flux_up = upwind(v + v_n, d, d_n)
            if flux_down is not None:
                u, t_s, g = get(step, 0, j), get(step, 2, j - 1), geo[j]
                cor = spin[j : j + 1, :]
                flux_x = upwind(u + east(u), d, east(d))
                new[0][j] = u - (east(g) - west(g)) + cor * v
                new[1][j] = v - (geo[j + 1] - geo[j - 1]) - cor * u
                new[2][j] = t - 0.05 * (u * (east(t) - west(t)) + v * (t_n - t_s))
                new[3][j] = d - 0.05 * (flux_x - west(flux_x) + flux_up - flux_down)
            flux_down = flux_up

        if step + 1 < 4:

            @pl.when(lat == 0)
            def _():
                for ref in new[1:]:
                    ref[:4] = jnp.zeros((4, width, LANES), jnp.float32)

            @pl.when(lat == lax.axis_size("lat") - 1)
            def _():
                for ref in new[1:]:
                    ref[8:] = jnp.zeros((4, width, LANES), jnp.float32)

    u, v, t, d = (ref[4:8, rim : rim + chunk, :] for ref in buffers[STEPS % 2])
    for f, q in enumerate((u * d, v * d, t * d, d)):
        result[4 * f : 4 * f + 4] = q
    flat = result[...].reshape(count * chunk, LANES)
    prefix = times_exact(flat, above, 3).reshape(count, chunk, LANES)
    lane = lax.broadcasted_iota(jnp.int32, (chunk, LANES), 1)
    for r in range(4):
        source = place[4 + r].astype(jnp.int32)
        part = place[r]
        for f in range(4):
            k = 4 * f + r
            mass = jnp.take_along_axis(prefix[k], source, axis=1) + part * jnp.take_along_axis(
                result[k], source, axis=1
            )
            result[k] = mass - jnp.where(lane == 0, 0.0, pltpu.roll(mass, 1, 1))
    for i in range(chunk // BLOCK):
        at = pl.ds(i * BLOCK, BLOCK)
        for s, tile in enumerate(scattered([result[k, at, :] for k in range(count)])):
            out_ref[s, at, :] = tile


def unpack_target(raw_ref, place):
    count, size, _ = raw_ref.shape
    half = place.shape[1] // 2
    for i in range(size // BLOCK):
        at = pl.ds(i * BLOCK, BLOCK)
        tiles = gathered([raw_ref[s, at, :] for s in range(count)])
        keep = min(BLOCK, half - i * BLOCK)
        for j in range(2):
            for k in range(8):
                start = j * half + i * BLOCK
                place[k, start : start + keep, :] = tiles[8 * j + k][:keep]


def receive_kernel(in_ref, *refs):
    outs, turned, flat = refs[:4], refs[4], refs[5]
    rows, _, lon = outs[0].shape
    count, chunk, _ = in_ref.shape
    mine = lax.axis_index("lev")
    for c in range(count):
        flat[c * chunk : (c + 1) * chunk, :] = in_ref[slot(c)]
    for at in range(0, lon, LANES):
        turned[:, :, at : at + LANES] = flat[at : at + LANES, :].T.reshape(count, BLOCK, LANES)
    for f, ref in enumerate(outs):
        for r in range(rows):
            ref[r] = turned[lax.rem(mine + rows * f + r, count)]


def call(kernel, ins, outs, scratch, *args, limit=24 * 2**20, flops=0, space=pltpu.VMEM):
    shapes = [jax.ShapeDtypeStruct(shape, jnp.float32) for shape in outs]
    moved = sum(4 * math.prod(a.shape) for a in (*args, *shapes))
    return pl.pallas_call(
        kernel,
        out_shape=shapes,
        in_specs=[pl.BlockSpec(memory_space=ins)] * len(args),
        out_specs=[pl.BlockSpec(memory_space=space)] * len(outs),
        scratch_shapes=[
            pltpu.VMEM(shape, jnp.float32) if isinstance(shape, tuple) else shape
            for shape in scratch
        ],
        cost_estimate=pl.CostEstimate(flops=flops, bytes_accessed=moved, transcendentals=0),
        compiler_params=pltpu.CompilerParams(vmem_limit_bytes=limit),
    )(*args)


def body(wind_east, wind_north, pot_temp, thickness, source_level, fraction):
    rows, depth, lon = wind_east.shape
    count = lax.axis_size("lev")
    blocks = lax.axis_size("lat")
    chunk = lon // count
    width = chunk + 2 * STEPS
    size = -(-(chunk // 2) // BLOCK) * BLOCK
    slab = wind_east.shape
    stack = (count, depth, lon)
    column = (count, chunk, LANES)
    (state,) = call(
        send_state, pltpu.HBM, [(count, width, LANES)],
        [stack, (lon + 2 * BLOCK, LANES)]
        + [pltpu.SemaphoreType.DMA((4 * rows,)), pltpu.SemaphoreType.DMA((count,))],
        wind_east, wind_north, pot_temp, thickness, limit=60 * 2**20, space=pltpu.HBM,
    )
    (target,) = call(
        send_target, pltpu.HBM, [(count, size, LANES)],
        [slab, pltpu.VMEM(slab, jnp.int32), stack, (lon + BLOCK, LANES)]
        + [pltpu.SemaphoreType.DMA((2,))],
        fraction, source_level, limit=60 * 2**20,
    )
    own = lax.all_to_all(state, "lev", 0, 0, tiled=True)
    own, target = lax.optimization_barrier((own, target))
    (own,) = call(unpack_state, pltpu.VMEM, [(count, width, LANES)], [], own)
    across = []
    for i in range(1, blocks - 1, 2):
        for k in range(count):
            m = k ^ 1 if i + 1 == blocks // 2 else k
            across += [(i * count + k, (i + 1) * count + m), ((i + 1) * count + m, i * count + k)]
    far = lax.ppermute(own, ("lat", "lev"), across)
    near = lax.ppermute(own, "lat", [(i, i ^ 1) for i in range(blocks)])
    target = lax.all_to_all(target, "lev", 0, 0, tiled=True)
    (place,) = call(unpack_target, pltpu.VMEM, [(8, chunk, LANES)], [], target, flops=2 * 10**10)
    (contents,) = call(
        core_kernel, pltpu.VMEM, [column],
        [(3 * rows, width, LANES)] * 9 + [(16, LANES), column],
        own, near, far, place, flops=3 * 10**8,
    )
    contents = lax.all_to_all(contents, "lev", 0, 0, tiled=True)
    return tuple(call(receive_kernel, pltpu.VMEM, [slab] * 4, [stack, (lon, LANES)], contents))


def solution(mesh):
    placed = P("lat", "lev", None)
    return jax.shard_map(
        body, mesh=mesh, in_specs=(placed,) * 6, out_specs=(placed,) * 4, check_vma=False
    )
```

```python
import math

import jax
import jax.numpy as jnp
from jax import lax
from jax.experimental import pallas as pl
from jax.experimental.pallas import tpu as pltpu
from jax.sharding import PartitionSpec as P

STEPS = 4
LANES = 128
BLOCK = 8
ORDER = [0, 1, 7, 6, 12, 13, 3, 2, 8, 9, 15, 14, 4, 5, 11, 10]
RANK = [ORDER.index(i) for i in range(len(ORDER))]


def exchange(x):
    return lax.all_to_all(x, "lev", 0, 0, tiled=True, axis_index_groups=[ORDER])


def slot(chunk):
    half = lax.axis_size("lat") // 2
    swapped = lax.div(lax.axis_index("lat"), half)
    return RANK[chunk] + swapped * (RANK[chunk ^ 1] - RANK[chunk])


def fetch(sources, targets, sems):
    copies = [
        pltpu.make_async_copy(source, target, sems.at[i])
        for i, (source, target) in enumerate(zip(sources, targets))
    ]
    for copy in copies:
        copy.start()
    return copies


def turn(stack, flat, base):
    lon = stack.shape[-1]
    for at in range(0, lon, LANES):
        flat[base + at : base + at + LANES, :] = (
            stack[:, :, at : at + LANES].reshape(LANES, LANES).T
        )


def send_state(u_in, v_in, t_in, d_in, state_out, stack, flat, in_sems, out_sems):
    rows, _, lon = u_in.shape
    count, width, _ = state_out.shape
    chunk = lon // count
    rim = (width - chunk) // 2
    mine = lax.axis_index("lev")
    places = [stack.at[lax.rem(mine + j, count)] for j in range(4 * rows)]
    sources = [ref.at[r] for ref in (u_in, v_in, t_in, d_in) for r in range(rows)]
    for copy in fetch(sources, places, in_sems):
        copy.wait()

    base = BLOCK + rim
    outs = [
        pltpu.make_async_copy(
            flat.at[pl.ds(BLOCK + c * chunk, width)], state_out.at[slot(c)], out_sems.at[c]
        )
        for c in range(count)
    ]
    sent = 1
    for at in range(0, lon, LANES):
        flat[base + at : base + at + LANES, :] = (
            stack[:, :, at : at + LANES].reshape(LANES, LANES).T
        )
        while sent < count - 1 and (sent + 1) * chunk + rim <= at + LANES:
            outs[sent].start()
            sent += 1
    flat[base - rim : base, :] = flat[base + lon - rim : base + lon, :]
    flat[base + lon :, :] = flat[base : base + rim, :]
    outs[0].start()
    for c in range(sent, count):
        outs[c].start()
    for copy in outs:
        copy.wait()


def send_target(f_in, s_in, target_ref, part, level, stack, flat, sems):
    rows, _, lon = f_in.shape
    count, size, _ = target_ref.shape
    chunk = lon // count
    half = chunk // 2
    mine = lax.axis_index("lev")
    for copy in fetch((f_in, s_in), (part, level), sems):
        copy.wait()
    for h in range(2):
        for r in range(rows):
            stack[lax.rem(mine + 8 * h + r, count)] = part[r]
            stack[lax.rem(mine + 8 * h + 4 + r, count)] = level[r].astype(jnp.float32)
    turn(stack, flat, 0)
    flat[lon:, :] = jnp.zeros((flat.shape[0] - lon, LANES), jnp.float32)
    place = lax.broadcasted_iota(jnp.int32, (size, LANES), 1) // BLOCK
    first = lax.rem(place - mine + count, count) < count // 2
    for c in range(count):
        at = c * chunk
        target_ref[slot(c)] = jnp.where(
            first, flat[at : at + size, :], flat[at + half : at + half + size, :]
        )


def spread(tiles):
    count = len(tiles)
    lane = lax.broadcasted_iota(jnp.int32, tiles[0].shape, 1) // BLOCK
    tiles = [tiles[(count - t) % count] for t in range(count)]
    bit = 1
    while bit < count:
        upper = (lane & bit) != 0
        tiles = [jnp.where(upper, tiles[t - bit], tiles[t]) for t in range(count)]
        bit *= 2
    return tiles


def gathered(tiles):
    return [
        z if t == 0 else pltpu.roll(z, LANES - BLOCK * t, 1) for t, z in enumerate(spread(tiles))
    ]


def scattered(tiles):
    return spread([x if t == 0 else pltpu.roll(x, BLOCK * t, 1) for t, x in enumerate(tiles)])


def times_exact(x, matrix, parts):
    total = None
    for part in range(parts):
        piece = x.astype(jnp.bfloat16)
        term = jnp.dot(piece, matrix, preferred_element_type=jnp.float32)
        total = term if total is None else total + term
        if part < parts - 1:
            x = x - piece.astype(jnp.float32)
    return total


def unpack_state(raw_ref, out_ref, far_ref):
    count, width, _ = raw_ref.shape
    odd = lax.rem(lax.axis_index("lat"), 2)
    for i in range(width // BLOCK):
        at = pl.ds(i * BLOCK, BLOCK)
        tiles = gathered([raw_ref[RANK[s], at, :] for s in range(count)])
        for k, tile in enumerate(tiles):
            out_ref[k, at, :] = tile
            if k < 3:
                tile = jnp.where(odd == 1, tiles[k + 1], tile)
            if k != 3:
                far_ref[k - (k > 3), at, :] = tile


def core_kernel(own_ref, near_ref, far_ref, place, out_ref, *scratch):
    buffers = (scratch[0:4], scratch[4:8])
    geo, spin, result = scratch[8:11]
    count, width, _ = own_ref.shape
    chunk = out_ref.shape[1]
    rim = (width - chunk) // 2
    lat = lax.axis_index("lat")
    lat_rows = lax.axis_size("lat") * 4
    rows = 12

    odd = lax.rem(lat, 2)
    for f in range(4):
        buffers[0][f][pl.ds(8 - 8 * odd, 4)] = near_ref[4 * f : 4 * f + 4]
        if f > 0:
            buffers[0][f][pl.ds(8 * odd, 4)] = far_ref[4 * f - 1 : 4 * f + 3]
    buffers[0][0][pl.ds(1 + 7 * odd, 3)] = far_ref[:3]

    def get(step, f, j):
        if step == 0 and 4 <= j < 8:
            return own_ref[4 * f + j - 4]
        return buffers[step % 2][f][j]

    row_level = lax.broadcasted_iota(jnp.int32, (LANES, LANES), 0)
    col_level = lax.broadcasted_iota(jnp.int32, (LANES, LANES), 1)
    below = jnp.where(row_level > col_level, 1.0, jnp.where(row_level == col_level, 0.5, 0.0))
    below = below.astype(jnp.bfloat16)
    above = jnp.where(row_level < col_level, 1.0, 0.0).astype(jnp.bfloat16)
    slope = 0.05 / math.sqrt(LANES)

    row_index = lax.broadcasted_iota(jnp.int32, (16, LANES), 0) + (lat * 4 - 4)
    angle = math.pi * ((row_index.astype(jnp.float32) + 0.5) / lat_rows - 0.5)
    spin[...] = 0.15 * jnp.sin(angle)

    def east(x):
        return pltpu.roll(x, width - 1, 0)

    def west(x):
        return pltpu.roll(x, 1, 0)

    def upwind(speed, behind, ahead):
        return speed * jnp.where(speed > 0.0, behind, ahead)

    for step in range(STEPS):
        new = buffers[1 - step % 2]
        size = rows - 2 * step
        span = range(step, rows - step)
        load = jnp.concatenate([get(step, 3, j) * get(step, 2, j) for j in span], axis=0)
        heights = slope * times_exact(load, below, 3)
        geo[step : rows - step] = heights.reshape(size, width, LANES)
        flux_down = None
        for j in span:
            v, t, d = (get(step, f, j) for f in (1, 2, 3))
            if j == rows - step - 1:
                break
            v_n, t_n, d_n = (get(step, f, j + 1) for f in (1, 2, 3))
            flux_up = upwind(v + v_n, d, d_n)
            if flux_down is not None:
                u, t_s, g = get(step, 0, j), get(step, 2, j - 1), geo[j]
                cor = spin[j : j + 1, :]
                flux_x = upwind(u + east(u), d, east(d))
                new[0][j] = u - (east(g) - west(g)) + cor * v
                new[1][j] = v - (geo[j + 1] - geo[j - 1]) - cor * u
                new[2][j] = t - 0.05 * (u * (east(t) - west(t)) + v * (t_n - t_s))
                new[3][j] = d - 0.05 * (flux_x - west(flux_x) + flux_up - flux_down)
            flux_down = flux_up

        if step + 1 < 4:

            @pl.when(lat == 0)
            def _():
                for ref in new[1:]:
                    ref[:4] = jnp.zeros((4, width, LANES), jnp.float32)

            @pl.when(lat == lax.axis_size("lat") - 1)
            def _():
                for ref in new[1:]:
                    ref[8:] = jnp.zeros((4, width, LANES), jnp.float32)

    u, v, t, d = (ref[4:8, rim : rim + chunk, :] for ref in buffers[STEPS % 2])
    for f, q in enumerate((u * d, v * d, t * d, d)):
        result[4 * f : 4 * f + 4] = q
    flat = result[...].reshape(count * chunk, LANES)
    prefix = times_exact(flat, above, 3).reshape(count, chunk, LANES)
    lane = lax.broadcasted_iota(jnp.int32, (BLOCK, LANES), 1)
    for i in range(chunk // BLOCK):
        at = slice(i * BLOCK, (i + 1) * BLOCK)
        tiles = [None] * count
        for r in range(4):
            source = place[4 + r, at, :].astype(jnp.int32)
            part = place[r, at, :]
            ks = range(r, count, 4)
            both = jnp.concatenate([prefix[k, at] for k in ks] + [result[k, at, :] for k in ks], axis=0)
            picked = jnp.take_along_axis(both, jnp.concatenate([source] * 8, axis=0), axis=1)
            for n, k in enumerate(ks):
                mass = picked[8 * n : 8 * n + 8] + part * picked[32 + 8 * n : 40 + 8 * n]
                tiles[k] = mass - jnp.where(lane == 0, 0.0, pltpu.roll(mass, 1, 1))
        for s, tile in enumerate(scattered(tiles)):
            out_ref[RANK[s], at, :] = tile


def unpack_target(raw_ref, place):
    count, size, _ = raw_ref.shape
    half = place.shape[1] // 2
    for i in range(size // BLOCK):
        at = pl.ds(i * BLOCK, BLOCK)
        tiles = gathered([raw_ref[RANK[s], at, :] for s in range(count)])
        keep = min(BLOCK, half - i * BLOCK)
        for j in range(2):
            for k in range(8):
                start = j * half + i * BLOCK
                place[k, start : start + keep, :] = tiles[8 * j + k][:keep]


def receive_kernel(in_ref, *refs):
    outs, turned, flat = refs[:4], refs[4], refs[5]
    rows, _, lon = outs[0].shape
    count, chunk, _ = in_ref.shape
    mine = lax.axis_index("lev")
    for c in range(count):
        flat[c * chunk : (c + 1) * chunk, :] = in_ref[slot(c)]
    for at in range(0, lon, LANES):
        turned[:, :, at : at + LANES] = flat[at : at + LANES, :].T.reshape(count, BLOCK, LANES)
    for f, ref in enumerate(outs):
        for r in range(rows):
            ref[r] = turned[lax.rem(mine + rows * f + r, count)]


def call(kernel, ins, outs, scratch, *args, limit=24 * 2**20, flops=0, space=pltpu.VMEM):
    shapes = [jax.ShapeDtypeStruct(shape, jnp.float32) for shape in outs]
    moved = sum(4 * math.prod(a.shape) for a in (*args, *shapes))
    return pl.pallas_call(
        kernel,
        out_shape=shapes,
        in_specs=[pl.BlockSpec(memory_space=ins)] * len(args),
        out_specs=[pl.BlockSpec(memory_space=space)] * len(outs),
        scratch_shapes=[
            pltpu.VMEM(shape, jnp.float32) if isinstance(shape, tuple) else shape
            for shape in scratch
        ],
        cost_estimate=pl.CostEstimate(flops=flops, bytes_accessed=moved, transcendentals=0),
        compiler_params=pltpu.CompilerParams(vmem_limit_bytes=limit),
    )(*args)


def body(wind_east, wind_north, pot_temp, thickness, source_level, fraction):
    rows, depth, lon = wind_east.shape
    count = lax.axis_size("lev")
    blocks = lax.axis_size("lat")
    chunk = lon // count
    width = chunk + 2 * STEPS
    size = -(-(chunk // 2) // BLOCK) * BLOCK
    slab = wind_east.shape
    stack = (count, depth, lon)
    column = (count, chunk, LANES)
    (state,) = call(
        send_state, pltpu.HBM, [(count, width, LANES)],
        [stack, (lon + 2 * BLOCK, LANES)]
        + [pltpu.SemaphoreType.DMA((4 * rows,)), pltpu.SemaphoreType.DMA((count,))],
        wind_east, wind_north, pot_temp, thickness, limit=60 * 2**20, space=pltpu.HBM,
    )
    (target,) = call(
        send_target, pltpu.HBM, [(count, size, LANES)],
        [slab, pltpu.VMEM(slab, jnp.int32), stack, (lon + BLOCK, LANES)]
        + [pltpu.SemaphoreType.DMA((2,))],
        fraction, source_level, limit=60 * 2**20,
    )
    own = exchange(state)
    own, target = lax.optimization_barrier((own, target))
    block = (count, width, LANES)
    own, edge = call(unpack_state, pltpu.VMEM, [block, (count - 1, *block[1:])], [], own)
    across = []
    for i in range(1, blocks - 1, 2):
        for k in range(count):
            m = k ^ 1 if i + 1 == blocks // 2 else k
            across += [(i * count + k, (i + 1) * count + m), ((i + 1) * count + m, i * count + k)]
    far = lax.ppermute(edge, ("lat", "lev"), across)
    near = lax.ppermute(own, "lat", [(i, i ^ 1) for i in range(blocks)])
    target = exchange(target)
    (place,) = call(unpack_target, pltpu.VMEM, [(8, chunk, LANES)], [], target, flops=2 * 10**10)
    (contents,) = call(
        core_kernel, pltpu.VMEM, [column],
        [(3 * rows, width, LANES)] * 9 + [(16, LANES), column],
        own, near, far, place, flops=3 * 10**8,
    )
    contents = exchange(contents)
    return tuple(call(receive_kernel, pltpu.VMEM, [slab] * 4, [stack, (lon, LANES)], contents))


def solution(mesh):
    placed = P("lat", "lev", None)
    return jax.shard_map(
        body, mesh=mesh, in_specs=(placed,) * 6, out_specs=(placed,) * 4, check_vma=False
    )
```

```python
import math

import jax
import jax.numpy as jnp
from jax import lax
from jax.experimental import pallas as pl
from jax.experimental.pallas import tpu as pltpu
from jax.sharding import PartitionSpec as P

STEPS = 4
LANES = 128
BLOCK = 8
ORDER = [8, 9, 15, 14, 4, 5, 11, 10, 0, 1, 7, 6, 12, 13, 3, 2]
RANK = [ORDER.index(i) for i in range(len(ORDER))]


def exchange(x):
    return lax.all_to_all(x, "lev", 0, 0, tiled=True, axis_index_groups=[ORDER])


def slot(chunk):
    half = lax.axis_size("lat") // 2
    swapped = lax.div(lax.axis_index("lat"), half)
    return RANK[chunk] + swapped * (RANK[chunk ^ 1] - RANK[chunk])


def fetch(sources, targets, sems):
    copies = [
        pltpu.make_async_copy(source, target, sems.at[i])
        for i, (source, target) in enumerate(zip(sources, targets))
    ]
    for copy in copies:
        copy.start()
    return copies


def turn(stack, flat, base):
    lon = stack.shape[-1]
    for at in range(0, lon, LANES):
        flat[base + at : base + at + LANES, :] = (
            stack[:, :, at : at + LANES].reshape(LANES, LANES).T
        )


def send_state(u_in, v_in, t_in, d_in, state_out, stack, flat, in_sems, out_sems):
    rows, _, lon = u_in.shape
    count, width, _ = state_out.shape
    chunk = lon // count
    rim = (width - chunk) // 2
    mine = lax.axis_index("lev")
    places = [stack.at[lax.rem(mine + j, count)] for j in range(4 * rows)]
    sources = [ref.at[r] for ref in (u_in, v_in, t_in, d_in) for r in range(rows)]
    for copy in fetch(sources, places, in_sems):
        copy.wait()

    base = BLOCK + rim
    outs = [
        pltpu.make_async_copy(
            flat.at[pl.ds(BLOCK + c * chunk, width)], state_out.at[slot(c)], out_sems.at[c]
        )
        for c in range(count)
    ]
    sent = 1
    for at in range(0, lon, LANES):
        flat[base + at : base + at + LANES, :] = (
            stack[:, :, at : at + LANES].reshape(LANES, LANES).T
        )
        while sent < count - 1 and (sent + 1) * chunk + rim <= at + LANES:
            outs[sent].start()
            sent += 1
    flat[base - rim : base, :] = flat[base + lon - rim : base + lon, :]
    flat[base + lon :, :] = flat[base : base + rim, :]
    outs[0].start()
    for c in range(sent, count):
        outs[c].start()
    for copy in outs:
        copy.wait()


def send_target(f_in, s_in, target_ref, part, level, stack, flat, sems):
    rows, _, lon = f_in.shape
    count, size, _ = target_ref.shape
    chunk = lon // count
    half = chunk // 2
    mine = lax.axis_index("lev")
    for copy in fetch((f_in, s_in), (part, level), sems):
        copy.wait()
    for h in range(2):
        for r in range(rows):
            stack[lax.rem(mine + 8 * h + r, count)] = part[r]
            stack[lax.rem(mine + 8 * h + 4 + r, count)] = level[r].astype(jnp.float32)
    turn(stack, flat, 0)
    flat[lon:, :] = jnp.zeros((flat.shape[0] - lon, LANES), jnp.float32)
    place = lax.broadcasted_iota(jnp.int32, (size, LANES), 1) // BLOCK
    first = lax.rem(place - mine + count, count) < count // 2
    for c in range(count):
        at = c * chunk
        target_ref[slot(c)] = jnp.where(
            first, flat[at : at + size, :], flat[at + half : at + half + size, :]
        )


def spread(tiles):
    count = len(tiles)
    lane = lax.broadcasted_iota(jnp.int32, tiles[0].shape, 1) // BLOCK
    tiles = [tiles[(count - t) % count] for t in range(count)]
    bit = 1
    while bit < count:
        upper = (lane & bit) != 0
        tiles = [jnp.where(upper, tiles[t - bit], tiles[t]) for t in range(count)]
        bit *= 2
    return tiles


def gathered(tiles):
    return [
        z if t == 0 else pltpu.roll(z, LANES - BLOCK * t, 1) for t, z in enumerate(spread(tiles))
    ]


def scattered(tiles):
    return spread([x if t == 0 else pltpu.roll(x, BLOCK * t, 1) for t, x in enumerate(tiles)])


def times_exact(x, matrix, parts):
    total = None
    for part in range(parts):
        piece = x.astype(jnp.bfloat16)
        term = jnp.dot(piece, matrix, preferred_element_type=jnp.float32)
        total = term if total is None else total + term
        if part < parts - 1:
            x = x - piece.astype(jnp.float32)
    return total


def unpack_state(raw_ref, out_ref, far_ref):
    count, width, _ = raw_ref.shape
    odd = lax.rem(lax.axis_index("lat"), 2)
    for i in range(width // BLOCK):
        at = pl.ds(i * BLOCK, BLOCK)
        tiles = gathered([raw_ref[RANK[s], at, :] for s in range(count)])
        for k, tile in enumerate(tiles):
            out_ref[k, at, :] = tile
            if k < 3:
                tile = jnp.where(odd == 1, tiles[k + 1], tile)
            if k != 3:
                far_ref[k - (k > 3), at, :] = tile


def core_kernel(own_ref, near_ref, far_ref, place, out_ref, *scratch):
    buffers = (scratch[0:4], scratch[4:8])
    geo, spin, result = scratch[8:11]
    count, width, _ = own_ref.shape
    chunk = out_ref.shape[1]
    rim = (width - chunk) // 2
    lat = lax.axis_index("lat")
    lat_rows = lax.axis_size("lat") * 4
    rows = 12

    odd = lax.rem(lat, 2)
    for f in range(4):
        buffers[0][f][pl.ds(8 - 8 * odd, 4)] = near_ref[4 * f : 4 * f + 4]
        if f > 0:
            buffers[0][f][pl.ds(8 * odd, 4)] = far_ref[4 * f - 1 : 4 * f + 3]
    buffers[0][0][pl.ds(1 + 7 * odd, 3)] = far_ref[:3]

    def get(step, f, j):
        if step == 0 and 4 <= j < 8:
            return own_ref[4 * f + j - 4]
        return buffers[step % 2][f][j]

    row_level = lax.broadcasted_iota(jnp.int32, (LANES, LANES), 0)
    col_level = lax.broadcasted_iota(jnp.int32, (LANES, LANES), 1)
    below = jnp.where(row_level > col_level, 1.0, jnp.where(row_level == col_level, 0.5, 0.0))
    below = below.astype(jnp.bfloat16)
    above = jnp.where(row_level < col_level, 1.0, 0.0).astype(jnp.bfloat16)
    slope = 0.05 / math.sqrt(LANES)

    row_index = lax.broadcasted_iota(jnp.int32, (16, LANES), 0) + (lat * 4 - 4)
    angle = math.pi * ((row_index.astype(jnp.float32) + 0.5) / lat_rows - 0.5)
    spin[...] = 0.15 * jnp.sin(angle)

    def east(x):
        return pltpu.roll(x, width - 1, 0)

    def west(x):
        return pltpu.roll(x, 1, 0)

    def upwind(speed, behind, ahead):
        return speed * jnp.where(speed > 0.0, behind, ahead)

    for step in range(STEPS):
        new = buffers[1 - step % 2]
        size = rows - 2 * step
        span = range(step, rows - step)
        load = jnp.concatenate([get(step, 3, j) * get(step, 2, j) for j in span], axis=0)
        heights = slope * times_exact(load, below, 3)
        geo[step : rows - step] = heights.reshape(size, width, LANES)
        flux_down = None
        for j in span:
            v, t, d = (get(step, f, j) for f in (1, 2, 3))
            if j == rows - step - 1:
                break
            v_n, t_n, d_n = (get(step, f, j + 1) for f in (1, 2, 3))
            flux_up = upwind(v + v_n, d, d_n)
            if flux_down is not None:
                u, t_s, g = get(step, 0, j), get(step, 2, j - 1), geo[j]
                cor = spin[j : j + 1, :]
                flux_x = upwind(u + east(u), d, east(d))
                new[0][j] = u - (east(g) - west(g)) + cor * v
                new[1][j] = v - (geo[j + 1] - geo[j - 1]) - cor * u
                new[2][j] = t - 0.05 * (u * (east(t) - west(t)) + v * (t_n - t_s))
                new[3][j] = d - 0.05 * (flux_x - west(flux_x) + flux_up - flux_down)
            flux_down = flux_up

        if step + 1 < 4:

            @pl.when(lat == 0)
            def _():
                for ref in new[1:]:
                    ref[:4] = jnp.zeros((4, width, LANES), jnp.float32)

            @pl.when(lat == lax.axis_size("lat") - 1)
            def _():
                for ref in new[1:]:
                    ref[8:] = jnp.zeros((4, width, LANES), jnp.float32)

    u, v, t, d = (ref[4:8, rim : rim + chunk, :] for ref in buffers[STEPS % 2])
    for f, q in enumerate((u * d, v * d, t * d, d)):
        result[4 * f : 4 * f + 4] = q
    flat = result[...].reshape(count * chunk, LANES)
    prefix = times_exact(flat, above, 3).reshape(count, chunk, LANES)
    lane = lax.broadcasted_iota(jnp.int32, (BLOCK, LANES), 1)
    for i in range(chunk // BLOCK):
        at = slice(i * BLOCK, (i + 1) * BLOCK)
        tiles = [None] * count
        for r in range(4):
            source = place[4 + r, at, :].astype(jnp.int32)
            part = place[r, at, :]
            ks = range(r, count, 4)
            both = jnp.concatenate([prefix[k, at] for k in ks] + [result[k, at, :] for k in ks], axis=0)
            picked = jnp.take_along_axis(both, jnp.concatenate([source] * 8, axis=0), axis=1)
            for n, k in enumerate(ks):
                mass = picked[8 * n : 8 * n + 8] + part * picked[32 + 8 * n : 40 + 8 * n]
                tiles[k] = mass - jnp.where(lane == 0, 0.0, pltpu.roll(mass, 1, 1))
        for s, tile in enumerate(scattered(tiles)):
            out_ref[RANK[s], at, :] = tile


def unpack_target(raw_ref, place):
    count, size, _ = raw_ref.shape
    half = place.shape[1] // 2
    for i in range(size // BLOCK):
        at = pl.ds(i * BLOCK, BLOCK)
        tiles = gathered([raw_ref[RANK[s], at, :] for s in range(count)])
        keep = min(BLOCK, half - i * BLOCK)
        for j in range(2):
            for k in range(8):
                start = j * half + i * BLOCK
                place[k, start : start + keep, :] = tiles[8 * j + k][:keep]


def receive_kernel(in_ref, *refs):
    outs, turned, flat = refs[:4], refs[4], refs[5]
    rows, _, lon = outs[0].shape
    count, chunk, _ = in_ref.shape
    mine = lax.axis_index("lev")
    for c in range(count):
        flat[c * chunk : (c + 1) * chunk, :] = in_ref[slot(c)]
    for at in range(0, lon, LANES):
        turned[:, :, at : at + LANES] = flat[at : at + LANES, :].T.reshape(count, BLOCK, LANES)
    for f, ref in enumerate(outs):
        for r in range(rows):
            ref[r] = turned[lax.rem(mine + rows * f + r, count)]


def call(kernel, ins, outs, scratch, *args, limit=24 * 2**20, flops=0, space=pltpu.VMEM):
    shapes = [jax.ShapeDtypeStruct(shape, jnp.float32) for shape in outs]
    moved = sum(4 * math.prod(a.shape) for a in (*args, *shapes))
    return pl.pallas_call(
        kernel,
        out_shape=shapes,
        in_specs=[pl.BlockSpec(memory_space=ins)] * len(args),
        out_specs=[pl.BlockSpec(memory_space=space)] * len(outs),
        scratch_shapes=[
            pltpu.VMEM(shape, jnp.float32) if isinstance(shape, tuple) else shape
            for shape in scratch
        ],
        cost_estimate=pl.CostEstimate(flops=flops, bytes_accessed=moved, transcendentals=0),
        compiler_params=pltpu.CompilerParams(vmem_limit_bytes=limit),
    )(*args)


def body(wind_east, wind_north, pot_temp, thickness, source_level, fraction):
    rows, depth, lon = wind_east.shape
    count = lax.axis_size("lev")
    blocks = lax.axis_size("lat")
    chunk = lon // count
    width = chunk + 2 * STEPS
    size = -(-(chunk // 2) // BLOCK) * BLOCK
    slab = wind_east.shape
    stack = (count, depth, lon)
    column = (count, chunk, LANES)
    (state,) = call(
        send_state, pltpu.HBM, [(count, width, LANES)],
        [stack, (lon + 2 * BLOCK, LANES)]
        + [pltpu.SemaphoreType.DMA((4 * rows,)), pltpu.SemaphoreType.DMA((count,))],
        wind_east, wind_north, pot_temp, thickness, limit=60 * 2**20, space=pltpu.HBM,
    )
    (target,) = call(
        send_target, pltpu.HBM, [(count, size, LANES)],
        [slab, pltpu.VMEM(slab, jnp.int32), stack, (lon + BLOCK, LANES)]
        + [pltpu.SemaphoreType.DMA((2,))],
        fraction, source_level, limit=60 * 2**20,
    )
    own = exchange(state)
    own, target = lax.optimization_barrier((own, target))
    block = (count, width, LANES)
    own, edge = call(unpack_state, pltpu.VMEM, [block, (count - 1, *block[1:])], [], own)
    across = []
    for i in range(1, blocks - 1, 2):
        for k in range(count):
            m = k ^ 1 if i + 1 == blocks // 2 else k
            across += [(i * count + k, (i + 1) * count + m), ((i + 1) * count + m, i * count + k)]
    far = lax.ppermute(edge, ("lat", "lev"), across)
    near = lax.ppermute(own, "lat", [(i, i ^ 1) for i in range(blocks)])
    target = exchange(target)
    (place,) = call(unpack_target, pltpu.VMEM, [(8, chunk, LANES)], [], target, flops=2 * 10**10)
    (contents,) = call(
        core_kernel, pltpu.VMEM, [column],
        [(3 * rows, width, LANES)] * 9 + [(16, LANES), column],
        own, near, far, place, flops=3 * 10**8,
    )
    contents = exchange(contents)
    return tuple(call(receive_kernel, pltpu.VMEM, [slab] * 4, [stack, (lon, LANES)], contents))


def solution(mesh):
    placed = P("lat", "lev", None)
    return jax.shard_map(
        body, mesh=mesh, in_specs=(placed,) * 6, out_specs=(placed,) * 4, check_vma=False
    )
```

```python
import math

import jax
import jax.numpy as jnp
from jax import lax
from jax.experimental import pallas as pl
from jax.experimental.pallas import tpu as pltpu
from jax.sharding import PartitionSpec as P

STEPS = 4
LANES = 128
BLOCK = 8
STATE_ORDER = [8, 9, 15, 14, 4, 5, 11, 10, 0, 1, 7, 6, 12, 13, 3, 2]
TARGET_ORDER = [0, 1, 7, 6, 12, 13, 3, 2, 8, 9, 15, 14, 4, 5, 11, 10]
RESULT_ORDER = [8, 9, 15, 14, 4, 5, 11, 10, 0, 1, 7, 6, 12, 13, 3, 2]


def rank(order):
    return [order.index(i) for i in range(len(order))]


def exchange(x, order):
    return lax.all_to_all(x, "lev", 0, 0, tiled=True, axis_index_groups=[order])


def slot(chunk, order):
    half = lax.axis_size("lat") // 2
    swapped = lax.div(lax.axis_index("lat"), half)
    places = rank(order)
    return places[chunk] + swapped * (places[chunk ^ 1] - places[chunk])


def fetch(sources, targets, sems):
    copies = [
        pltpu.make_async_copy(source, target, sems.at[i])
        for i, (source, target) in enumerate(zip(sources, targets))
    ]
    for copy in copies:
        copy.start()
    return copies


def turn(stack, flat, base):
    lon = stack.shape[-1]
    for at in range(0, lon, LANES):
        flat[base + at : base + at + LANES, :] = (
            stack[:, :, at : at + LANES].reshape(LANES, LANES).T
        )


def send_state(u_in, v_in, t_in, d_in, state_out, stack, flat, in_sems, out_sems):
    rows, _, lon = u_in.shape
    count, width, _ = state_out.shape
    chunk = lon // count
    rim = (width - chunk) // 2
    mine = lax.axis_index("lev")
    places = [stack.at[lax.rem(mine + j, count)] for j in range(4 * rows)]
    sources = [ref.at[r] for ref in (u_in, v_in, t_in, d_in) for r in range(rows)]
    for copy in fetch(sources, places, in_sems):
        copy.wait()

    base = BLOCK + rim
    outs = [
        pltpu.make_async_copy(
            flat.at[pl.ds(BLOCK + c * chunk, width)], state_out.at[slot(c, STATE_ORDER)], out_sems.at[c]
        )
        for c in range(count)
    ]
    sent = 1
    for at in range(0, lon, LANES):
        flat[base + at : base + at + LANES, :] = (
            stack[:, :, at : at + LANES].reshape(LANES, LANES).T
        )
        while sent < count - 1 and (sent + 1) * chunk + rim <= at + LANES:
            outs[sent].start()
            sent += 1
    flat[base - rim : base, :] = flat[base + lon - rim : base + lon, :]
    flat[base + lon :, :] = flat[base : base + rim, :]
    outs[0].start()
    for c in range(sent, count):
        outs[c].start()
    for copy in outs:
        copy.wait()


def send_target(f_in, s_in, target_ref, part, level, stack, flat, sems):
    rows, _, lon = f_in.shape
    count, size, _ = target_ref.shape
    chunk = lon // count
    half = chunk // 2
    mine = lax.axis_index("lev")
    for copy in fetch((f_in, s_in), (part, level), sems):
        copy.wait()
    for h in range(2):
        for r in range(rows):
            stack[lax.rem(mine + 8 * h + r, count)] = part[r]
            stack[lax.rem(mine + 8 * h + 4 + r, count)] = level[r].astype(jnp.float32)
    turn(stack, flat, 0)
    flat[lon:, :] = jnp.zeros((flat.shape[0] - lon, LANES), jnp.float32)
    place = lax.broadcasted_iota(jnp.int32, (size, LANES), 1) // BLOCK
    first = lax.rem(place - mine + count, count) < count // 2
    for c in range(count):
        at = c * chunk
        target_ref[slot(c, TARGET_ORDER)] = jnp.where(
            first, flat[at : at + size, :], flat[at + half : at + half + size, :]
        )


def spread(tiles):
    count = len(tiles)
    lane = lax.broadcasted_iota(jnp.int32, tiles[0].shape, 1) // BLOCK
    tiles = [tiles[(count - t) % count] for t in range(count)]
    bit = 1
    while bit < count:
        upper = (lane & bit) != 0
        tiles = [jnp.where(upper, tiles[t - bit], tiles[t]) for t in range(count)]
        bit *= 2
    return tiles


def gathered(tiles):
    return [
        z if t == 0 else pltpu.roll(z, LANES - BLOCK * t, 1) for t, z in enumerate(spread(tiles))
    ]


def scattered(tiles):
    return spread([x if t == 0 else pltpu.roll(x, BLOCK * t, 1) for t, x in enumerate(tiles)])


def times_exact(x, matrix, parts):
    total = None
    for part in range(parts):
        piece = x.astype(jnp.bfloat16)
        term = jnp.dot(piece, matrix, preferred_element_type=jnp.float32)
        total = term if total is None else total + term
        if part < parts - 1:
            x = x - piece.astype(jnp.float32)
    return total


def unpack_state(raw_ref, out_ref, far_ref):
    count, width, _ = raw_ref.shape
    odd = lax.rem(lax.axis_index("lat"), 2)
    for i in range(width // BLOCK):
        at = pl.ds(i * BLOCK, BLOCK)
        tiles = gathered([raw_ref[s, at, :] for s in rank(STATE_ORDER)])
        for k, tile in enumerate(tiles):
            out_ref[k, at, :] = tile
            if k < 3:
                tile = jnp.where(odd == 1, tiles[k + 1], tile)
            if k != 3:
                far_ref[k - (k > 3), at, :] = tile


def core_kernel(own_ref, near_ref, far_ref, place, out_ref, *scratch):
    buffers = (scratch[0:4], scratch[4:8])
    geo, spin, result = scratch[8:11]
    count, width, _ = own_ref.shape
    chunk = out_ref.shape[1]
    rim = (width - chunk) // 2
    lat = lax.axis_index("lat")
    lat_rows = lax.axis_size("lat") * 4
    rows = 12

    odd = lax.rem(lat, 2)
    for f in range(4):
        buffers[0][f][pl.ds(8 - 8 * odd, 4)] = near_ref[4 * f : 4 * f + 4]
        if f > 0:
            buffers[0][f][pl.ds(8 * odd, 4)] = far_ref[4 * f - 1 : 4 * f + 3]
    buffers[0][0][pl.ds(1 + 7 * odd, 3)] = far_ref[:3]

    def get(step, f, j):
        if step == 0 and 4 <= j < 8:
            return own_ref[4 * f + j - 4]
        return buffers[step % 2][f][j]

    row_level = lax.broadcasted_iota(jnp.int32, (LANES, LANES), 0)
    col_level = lax.broadcasted_iota(jnp.int32, (LANES, LANES), 1)
    below = jnp.where(row_level > col_level, 1.0, jnp.where(row_level == col_level, 0.5, 0.0))
    below = below.astype(jnp.bfloat16)
    above = jnp.where(row_level < col_level, 1.0, 0.0).astype(jnp.bfloat16)
    slope = 0.05 / math.sqrt(LANES)

    row_index = lax.broadcasted_iota(jnp.int32, (16, LANES), 0) + (lat * 4 - 4)
    angle = math.pi * ((row_index.astype(jnp.float32) + 0.5) / lat_rows - 0.5)
    spin[...] = 0.15 * jnp.sin(angle)

    def east(x):
        return pltpu.roll(x, width - 1, 0)

    def west(x):
        return pltpu.roll(x, 1, 0)

    def upwind(speed, behind, ahead):
        return speed * jnp.where(speed > 0.0, behind, ahead)

    for step in range(STEPS):
        new = buffers[1 - step % 2]
        size = rows - 2 * step
        span = range(step, rows - step)
        load = jnp.concatenate([get(step, 3, j) * get(step, 2, j) for j in span], axis=0)
        heights = slope * times_exact(load, below, 3)
        geo[step : rows - step] = heights.reshape(size, width, LANES)
        flux_down = None
        for j in span:
            v, t, d = (get(step, f, j) for f in (1, 2, 3))
            if j == rows - step - 1:
                break
            v_n, t_n, d_n = (get(step, f, j + 1) for f in (1, 2, 3))
            flux_up = upwind(v + v_n, d, d_n)
            if flux_down is not None:
                u, t_s, g = get(step, 0, j), get(step, 2, j - 1), geo[j]
                cor = spin[j : j + 1, :]
                flux_x = upwind(u + east(u), d, east(d))
                new[0][j] = u - (east(g) - west(g)) + cor * v
                new[1][j] = v - (geo[j + 1] - geo[j - 1]) - cor * u
                new[2][j] = t - 0.05 * (u * (east(t) - west(t)) + v * (t_n - t_s))
                new[3][j] = d - 0.05 * (flux_x - west(flux_x) + flux_up - flux_down)
            flux_down = flux_up

        if step + 1 < 4:

            @pl.when(lat == 0)
            def _():
                for ref in new[1:]:
                    ref[:4] = jnp.zeros((4, width, LANES), jnp.float32)

            @pl.when(lat == lax.axis_size("lat") - 1)
            def _():
                for ref in new[1:]:
                    ref[8:] = jnp.zeros((4, width, LANES), jnp.float32)

    u, v, t, d = (ref[4:8, rim : rim + chunk, :] for ref in buffers[STEPS % 2])
    for f, q in enumerate((u * d, v * d, t * d, d)):
        result[4 * f : 4 * f + 4] = q
    flat = result[...].reshape(count * chunk, LANES)
    prefix = times_exact(flat, above, 3).reshape(count, chunk, LANES)
    lane = lax.broadcasted_iota(jnp.int32, (BLOCK, LANES), 1)
    for i in range(chunk // BLOCK):
        at = slice(i * BLOCK, (i + 1) * BLOCK)
        tiles = [None] * count
        for r in range(4):
            source = place[4 + r, at, :].astype(jnp.int32)
            part = place[r, at, :]
            ks = range(r, count, 4)
            both = jnp.concatenate([prefix[k, at] for k in ks] + [result[k, at, :] for k in ks], axis=0)
            picked = jnp.take_along_axis(both, jnp.concatenate([source] * 8, axis=0), axis=1)
            for n, k in enumerate(ks):
                mass = picked[8 * n : 8 * n + 8] + part * picked[32 + 8 * n : 40 + 8 * n]
                tiles[k] = mass - jnp.where(lane == 0, 0.0, pltpu.roll(mass, 1, 1))
        for s, tile in enumerate(scattered(tiles)):
            out_ref[rank(RESULT_ORDER)[s], at, :] = tile


def unpack_target(raw_ref, place):
    count, size, _ = raw_ref.shape
    half = place.shape[1] // 2
    for i in range(size // BLOCK):
        at = pl.ds(i * BLOCK, BLOCK)
        tiles = gathered([raw_ref[s, at, :] for s in rank(TARGET_ORDER)])
        keep = min(BLOCK, half - i * BLOCK)
        for j in range(2):
            for k in range(8):
                start = j * half + i * BLOCK
                place[k, start : start + keep, :] = tiles[8 * j + k][:keep]


def receive_kernel(in_ref, *refs):
    outs, turned, flat = refs[:4], refs[4], refs[5]
    rows, _, lon = outs[0].shape
    count, chunk, _ = in_ref.shape
    mine = lax.axis_index("lev")
    for c in range(count):
        flat[c * chunk : (c + 1) * chunk, :] = in_ref[slot(c, RESULT_ORDER)]
    for at in range(0, lon, LANES):
        turned[:, :, at : at + LANES] = flat[at : at + LANES, :].T.reshape(count, BLOCK, LANES)
    for f, ref in enumerate(outs):
        for r in range(rows):
            ref[r] = turned[lax.rem(mine + rows * f + r, count)]


def call(kernel, ins, outs, scratch, *args, limit=24 * 2**20, flops=0, space=pltpu.VMEM):
    shapes = [jax.ShapeDtypeStruct(shape, jnp.float32) for shape in outs]
    moved = sum(4 * math.prod(a.shape) for a in (*args, *shapes))
    return pl.pallas_call(
        kernel,
        out_shape=shapes,
        in_specs=[pl.BlockSpec(memory_space=ins)] * len(args),
        out_specs=[pl.BlockSpec(memory_space=space)] * len(outs),
        scratch_shapes=[
            pltpu.VMEM(shape, jnp.float32) if isinstance(shape, tuple) else shape
            for shape in scratch
        ],
        cost_estimate=pl.CostEstimate(flops=flops, bytes_accessed=moved, transcendentals=0),
        compiler_params=pltpu.CompilerParams(vmem_limit_bytes=limit),
    )(*args)


def body(wind_east, wind_north, pot_temp, thickness, source_level, fraction):
    rows, depth, lon = wind_east.shape
    count = lax.axis_size("lev")
    blocks = lax.axis_size("lat")
    chunk = lon // count
    width = chunk + 2 * STEPS
    size = -(-(chunk // 2) // BLOCK) * BLOCK
    slab = wind_east.shape
    stack = (count, depth, lon)
    column = (count, chunk, LANES)
    (state,) = call(
        send_state, pltpu.HBM, [(count, width, LANES)],
        [stack, (lon + 2 * BLOCK, LANES)]
        + [pltpu.SemaphoreType.DMA((4 * rows,)), pltpu.SemaphoreType.DMA((count,))],
        wind_east, wind_north, pot_temp, thickness, limit=60 * 2**20, space=pltpu.HBM,
    )
    (target,) = call(
        send_target, pltpu.HBM, [(count, size, LANES)],
        [slab, pltpu.VMEM(slab, jnp.int32), stack, (lon + BLOCK, LANES)]
        + [pltpu.SemaphoreType.DMA((2,))],
        fraction, source_level, limit=60 * 2**20,
    )
    own = exchange(state, STATE_ORDER)
    own, target = lax.optimization_barrier((own, target))
    block = (count, width, LANES)
    own, edge = call(unpack_state, pltpu.VMEM, [block, (count - 1, *block[1:])], [], own)
    across = []
    for i in range(1, blocks - 1, 2):
        for k in range(count):
            m = k ^ 1 if i + 1 == blocks // 2 else k
            across += [(i * count + k, (i + 1) * count + m), ((i + 1) * count + m, i * count + k)]
    far = lax.ppermute(edge, ("lat", "lev"), across)
    near = lax.ppermute(own, "lat", [(i, i ^ 1) for i in range(blocks)])
    target = exchange(target, TARGET_ORDER)
    (place,) = call(unpack_target, pltpu.VMEM, [(8, chunk, LANES)], [], target, flops=2 * 10**10)
    (contents,) = call(
        core_kernel, pltpu.VMEM, [column],
        [(3 * rows, width, LANES)] * 9 + [(16, LANES), column],
        own, near, far, place, flops=3 * 10**8,
    )
    contents = exchange(contents, RESULT_ORDER)
    return tuple(call(receive_kernel, pltpu.VMEM, [slab] * 4, [stack, (lon, LANES)], contents))


def solution(mesh):
    placed = P("lat", "lev", None)
    return jax.shard_map(
        body, mesh=mesh, in_specs=(placed,) * 6, out_specs=(placed,) * 4, check_vma=False
    )
```

```python
import math

import jax
import jax.numpy as jnp
from jax import lax
from jax.experimental import pallas as pl
from jax.experimental.pallas import tpu as pltpu
from jax.sharding import PartitionSpec as P

STEPS = 4
LANES = 128
BLOCK = 8
STATE_ORDER = [8, 9, 15, 14, 4, 5, 11, 10, 0, 1, 7, 6, 12, 13, 3, 2]
TARGET_ORDER = [0, 1, 9, 8, 4, 5, 13, 12, 2, 3, 11, 10, 6, 7, 15, 14]
RESULT_ORDER = [8, 9, 15, 14, 4, 5, 11, 10, 0, 1, 7, 6, 12, 13, 3, 2]


def rank(order):
    return [order.index(i) for i in range(len(order))]


def exchange(x, order):
    return lax.all_to_all(x, "lev", 0, 0, tiled=True, axis_index_groups=[order])


def slot(chunk, order):
    half = lax.axis_size("lat") // 2
    swapped = lax.div(lax.axis_index("lat"), half)
    places = rank(order)
    return places[chunk] + swapped * (places[chunk ^ 1] - places[chunk])


def fetch(sources, targets, sems):
    copies = [
        pltpu.make_async_copy(source, target, sems.at[i])
        for i, (source, target) in enumerate(zip(sources, targets))
    ]
    for copy in copies:
        copy.start()
    return copies


def turn(stack, flat, base):
    lon = stack.shape[-1]
    for at in range(0, lon, LANES):
        flat[base + at : base + at + LANES, :] = (
            stack[:, :, at : at + LANES].reshape(LANES, LANES).T
        )


def send_state(u_in, v_in, t_in, d_in, state_out, stack, flat, in_sems, out_sems):
    rows, _, lon = u_in.shape
    count, width, _ = state_out.shape
    chunk = lon // count
    rim = (width - chunk) // 2
    mine = lax.axis_index("lev")
    places = [stack.at[lax.rem(mine + j, count)] for j in range(4 * rows)]
    sources = [ref.at[r] for ref in (u_in, v_in, t_in, d_in) for r in range(rows)]
    for copy in fetch(sources, places, in_sems):
        copy.wait()

    base = BLOCK + rim
    outs = [
        pltpu.make_async_copy(
            flat.at[pl.ds(BLOCK + c * chunk, width)], state_out.at[slot(c, STATE_ORDER)], out_sems.at[c]
        )
        for c in range(count)
    ]
    sent = 1
    for at in range(0, lon, LANES):
        flat[base + at : base + at + LANES, :] = (
            stack[:, :, at : at + LANES].reshape(LANES, LANES).T
        )
        while sent < count - 1 and (sent + 1) * chunk + rim <= at + LANES:
            outs[sent].start()
            sent += 1
    flat[base - rim : base, :] = flat[base + lon - rim : base + lon, :]
    flat[base + lon :, :] = flat[base : base + rim, :]
    outs[0].start()
    for c in range(sent, count):
        outs[c].start()
    for copy in outs:
        copy.wait()


def send_target(f_in, s_in, target_ref, part, level, stack, flat, sems):
    rows, _, lon = f_in.shape
    count, size, _ = target_ref.shape
    chunk = lon // count
    half = chunk // 2
    mine = lax.axis_index("lev")
    for copy in fetch((f_in, s_in), (part, level), sems):
        copy.wait()
    for h in range(2):
        for r in range(rows):
            stack[lax.rem(mine + 8 * h + r, count)] = part[r]
            stack[lax.rem(mine + 8 * h + 4 + r, count)] = level[r].astype(jnp.float32)
    turn(stack, flat, 0)
    flat[lon:, :] = jnp.zeros((flat.shape[0] - lon, LANES), jnp.float32)
    place = lax.broadcasted_iota(jnp.int32, (size, LANES), 1) // BLOCK
    first = lax.rem(place - mine + count, count) < count // 2
    for c in range(count):
        at = c * chunk
        target_ref[slot(c, TARGET_ORDER)] = jnp.where(
            first, flat[at : at + size, :], flat[at + half : at + half + size, :]
        )


def spread(tiles):
    count = len(tiles)
    lane = lax.broadcasted_iota(jnp.int32, tiles[0].shape, 1) // BLOCK
    tiles = [tiles[(count - t) % count] for t in range(count)]
    bit = 1
    while bit < count:
        upper = (lane & bit) != 0
        tiles = [jnp.where(upper, tiles[t - bit], tiles[t]) for t in range(count)]
        bit *= 2
    return tiles


def gathered(tiles):
    return [
        z if t == 0 else pltpu.roll(z, LANES - BLOCK * t, 1) for t, z in enumerate(spread(tiles))
    ]


def scattered(tiles):
    return spread([x if t == 0 else pltpu.roll(x, BLOCK * t, 1) for t, x in enumerate(tiles)])


def times_exact(x, matrix, parts):
    total = None
    for part in range(parts):
        piece = x.astype(jnp.bfloat16)
        term = jnp.dot(piece, matrix, preferred_element_type=jnp.float32)
        total = term if total is None else total + term
        if part < parts - 1:
            x = x - piece.astype(jnp.float32)
    return total


def unpack_state(raw_ref, out_ref, far_ref):
    count, width, _ = raw_ref.shape
    odd = lax.rem(lax.axis_index("lat"), 2)
    for i in range(width // BLOCK):
        at = pl.ds(i * BLOCK, BLOCK)
        tiles = gathered([raw_ref[s, at, :] for s in rank(STATE_ORDER)])
        for k, tile in enumerate(tiles):
            out_ref[k, at, :] = tile
            if k < 3:
                tile = jnp.where(odd == 1, tiles[k + 1], tile)
            if k != 3:
                far_ref[k - (k > 3), at, :] = tile


def core_kernel(own_ref, near_ref, far_ref, place, out_ref, *scratch):
    buffers = (scratch[0:4], scratch[4:8])
    geo, spin, result = scratch[8:11]
    count, width, _ = own_ref.shape
    chunk = out_ref.shape[1]
    rim = (width - chunk) // 2
    lat = lax.axis_index("lat")
    lat_rows = lax.axis_size("lat") * 4
    rows = 12

    odd = lax.rem(lat, 2)
    for f in range(4):
        buffers[0][f][pl.ds(8 - 8 * odd, 4)] = near_ref[4 * f : 4 * f + 4]
        if f > 0:
            buffers[0][f][pl.ds(8 * odd, 4)] = far_ref[4 * f - 1 : 4 * f + 3]
    buffers[0][0][pl.ds(1 + 7 * odd, 3)] = far_ref[:3]

    def get(step, f, j):
        if step == 0 and 4 <= j < 8:
            return own_ref[4 * f + j - 4]
        return buffers[step % 2][f][j]

    row_level = lax.broadcasted_iota(jnp.int32, (LANES, LANES), 0)
    col_level = lax.broadcasted_iota(jnp.int32, (LANES, LANES), 1)
    below = jnp.where(row_level > col_level, 1.0, jnp.where(row_level == col_level, 0.5, 0.0))
    below = below.astype(jnp.bfloat16)
    above = jnp.where(row_level < col_level, 1.0, 0.0).astype(jnp.bfloat16)
    slope = 0.05 / math.sqrt(LANES)

    row_index = lax.broadcasted_iota(jnp.int32, (16, LANES), 0) + (lat * 4 - 4)
    angle = math.pi * ((row_index.astype(jnp.float32) + 0.5) / lat_rows - 0.5)
    spin[...] = 0.15 * jnp.sin(angle)

    def east(x):
        return pltpu.roll(x, width - 1, 0)

    def west(x):
        return pltpu.roll(x, 1, 0)

    def upwind(speed, behind, ahead):
        return speed * jnp.where(speed > 0.0, behind, ahead)

    for step in range(STEPS):
        new = buffers[1 - step % 2]
        size = rows - 2 * step
        span = range(step, rows - step)
        load = jnp.concatenate([get(step, 3, j) * get(step, 2, j) for j in span], axis=0)
        heights = slope * times_exact(load, below, 3)
        geo[step : rows - step] = heights.reshape(size, width, LANES)
        flux_down = None
        for j in span:
            v, t, d = (get(step, f, j) for f in (1, 2, 3))
            if j == rows - step - 1:
                break
            v_n, t_n, d_n = (get(step, f, j + 1) for f in (1, 2, 3))
            flux_up = upwind(v + v_n, d, d_n)
            if flux_down is not None:
                u, t_s, g = get(step, 0, j), get(step, 2, j - 1), geo[j]
                cor = spin[j : j + 1, :]
                flux_x = upwind(u + east(u), d, east(d))
                new[0][j] = u - (east(g) - west(g)) + cor * v
                new[1][j] = v - (geo[j + 1] - geo[j - 1]) - cor * u
                new[2][j] = t - 0.05 * (u * (east(t) - west(t)) + v * (t_n - t_s))
                new[3][j] = d - 0.05 * (flux_x - west(flux_x) + flux_up - flux_down)
            flux_down = flux_up

        if step + 1 < 4:

            @pl.when(lat == 0)
            def _():
                for ref in new[1:]:
                    ref[:4] = jnp.zeros((4, width, LANES), jnp.float32)

            @pl.when(lat == lax.axis_size("lat") - 1)
            def _():
                for ref in new[1:]:
                    ref[8:] = jnp.zeros((4, width, LANES), jnp.float32)

    u, v, t, d = (ref[4:8, rim : rim + chunk, :] for ref in buffers[STEPS % 2])
    for f, q in enumerate((u * d, v * d, t * d, d)):
        result[4 * f : 4 * f + 4] = q
    flat = result[...].reshape(count * chunk, LANES)
    prefix = times_exact(flat, above, 3).reshape(count, chunk, LANES)
    lane = lax.broadcasted_iota(jnp.int32, (BLOCK, LANES), 1)
    for i in range(chunk // BLOCK):
        at = slice(i * BLOCK, (i + 1) * BLOCK)
        tiles = [None] * count
        for r in range(4):
            source = place[4 + r, at, :].astype(jnp.int32)
            part = place[r, at, :]
            ks = range(r, count, 4)
            both = jnp.concatenate([prefix[k, at] for k in ks] + [result[k, at, :] for k in ks], axis=0)
            picked = jnp.take_along_axis(both, jnp.concatenate([source] * 8, axis=0), axis=1)
            for n, k in enumerate(ks):
                mass = picked[8 * n : 8 * n + 8] + part * picked[32 + 8 * n : 40 + 8 * n]
                tiles[k] = mass - jnp.where(lane == 0, 0.0, pltpu.roll(mass, 1, 1))
        for s, tile in enumerate(scattered(tiles)):
            out_ref[rank(RESULT_ORDER)[s], at, :] = tile


def unpack_target(raw_ref, place):
    count, size, _ = raw_ref.shape
    half = place.shape[1] // 2
    for i in range(size // BLOCK):
        at = pl.ds(i * BLOCK, BLOCK)
        tiles = gathered([raw_ref[s, at, :] for s in rank(TARGET_ORDER)])
        keep = min(BLOCK, half - i * BLOCK)
        for j in range(2):
            for k in range(8):
                start = j * half + i * BLOCK
                place[k, start : start + keep, :] = tiles[8 * j + k][:keep]


def receive_kernel(in_ref, *refs):
    outs, turned, flat = refs[:4], refs[4], refs[5]
    rows, _, lon = outs[0].shape
    count, chunk, _ = in_ref.shape
    mine = lax.axis_index("lev")
    for c in range(count):
        flat[c * chunk : (c + 1) * chunk, :] = in_ref[slot(c, RESULT_ORDER)]
    for at in range(0, lon, LANES):
        turned[:, :, at : at + LANES] = flat[at : at + LANES, :].T.reshape(count, BLOCK, LANES)
    for f, ref in enumerate(outs):
        for r in range(rows):
            ref[r] = turned[lax.rem(mine + rows * f + r, count)]


def call(kernel, ins, outs, scratch, *args, limit=24 * 2**20, flops=0, space=pltpu.VMEM):
    shapes = [jax.ShapeDtypeStruct(shape, jnp.float32) for shape in outs]
    moved = sum(4 * math.prod(a.shape) for a in (*args, *shapes))
    return pl.pallas_call(
        kernel,
        out_shape=shapes,
        in_specs=[pl.BlockSpec(memory_space=ins)] * len(args),
        out_specs=[pl.BlockSpec(memory_space=space)] * len(outs),
        scratch_shapes=[
            pltpu.VMEM(shape, jnp.float32) if isinstance(shape, tuple) else shape
            for shape in scratch
        ],
        cost_estimate=pl.CostEstimate(flops=flops, bytes_accessed=moved, transcendentals=0),
        compiler_params=pltpu.CompilerParams(vmem_limit_bytes=limit),
    )(*args)


def body(wind_east, wind_north, pot_temp, thickness, source_level, fraction):
    rows, depth, lon = wind_east.shape
    count = lax.axis_size("lev")
    blocks = lax.axis_size("lat")
    chunk = lon // count
    width = chunk + 2 * STEPS
    size = -(-(chunk // 2) // BLOCK) * BLOCK
    slab = wind_east.shape
    stack = (count, depth, lon)
    column = (count, chunk, LANES)
    (state,) = call(
        send_state, pltpu.HBM, [(count, width, LANES)],
        [stack, (lon + 2 * BLOCK, LANES)]
        + [pltpu.SemaphoreType.DMA((4 * rows,)), pltpu.SemaphoreType.DMA((count,))],
        wind_east, wind_north, pot_temp, thickness, limit=60 * 2**20, space=pltpu.HBM,
    )
    (target,) = call(
        send_target, pltpu.HBM, [(count, size, LANES)],
        [slab, pltpu.VMEM(slab, jnp.int32), stack, (lon + BLOCK, LANES)]
        + [pltpu.SemaphoreType.DMA((2,))],
        fraction, source_level, limit=60 * 2**20,
    )
    own = exchange(state, STATE_ORDER)
    own, target = lax.optimization_barrier((own, target))
    block = (count, width, LANES)
    own, edge = call(unpack_state, pltpu.VMEM, [block, (count - 1, *block[1:])], [], own)
    across = []
    for i in range(1, blocks - 1, 2):
        for k in range(count):
            m = k ^ 1 if i + 1 == blocks // 2 else k
            across += [(i * count + k, (i + 1) * count + m), ((i + 1) * count + m, i * count + k)]
    far = lax.ppermute(edge, ("lat", "lev"), across)
    near = lax.ppermute(own, "lat", [(i, i ^ 1) for i in range(blocks)])
    target = exchange(target, TARGET_ORDER)
    (place,) = call(unpack_target, pltpu.VMEM, [(8, chunk, LANES)], [], target, flops=2 * 10**10)
    (contents,) = call(
        core_kernel, pltpu.VMEM, [column],
        [(3 * rows, width, LANES)] * 9 + [(16, LANES), column],
        own, near, far, place, flops=3 * 10**8,
    )
    contents = exchange(contents, RESULT_ORDER)
    return tuple(call(receive_kernel, pltpu.VMEM, [slab] * 4, [stack, (lon, LANES)], contents))


def solution(mesh):
    placed = P("lat", "lev", None)
    return jax.shard_map(
        body, mesh=mesh, in_specs=(placed,) * 6, out_specs=(placed,) * 4, check_vma=False
    )
```
